256 devices in a mesh: dp: 4 (over y), tm: 8 (over z_lo, core), patch: 8 (over z_hi, x).
Axes of the slice: x: 4, y: 4, z: 8 (z_hi: 2, z_lo: 4; z = z_hi * 4 + z_lo), core: 2. Of those that a mesh axis runs over, the one named last changes fastest.
Arguments:
- inputs: bfloat16 [4, 16, 512, 2048], P('dp', 'tm', 'patch'), may hold values from -24 to 24
- w_query: bfloat16 [2048, 1024], P(None, 'patch'), may hold values from -0.125 to 0.125
- w_key: bfloat16 [2048, 1024], P(None, 'patch'), may hold values from -0.125 to 0.125
- w_value: bfloat16 [2048, 1024], P(None, 'patch'), may hold values from -0.125 to 0.125
- w_out: bfloat16 [1024, 2048], P('patch'), may hold values from -0.1875 to 0.1875
- grad_out: bfloat16 [4, 16, 512, 2048], P('dp', 'tm', 'patch'), may hold values from -6 to 6
Outputs:
- grad_inputs: bfloat16 [4, 16, 512, 2048], P('dp', 'tm', 'patch')
- grad_w_query: float32 [2048, 1024], P(('dp', 'tm'), 'patch')
- grad_w_key: float32 [2048, 1024], P(('dp', 'tm'), 'patch')
- grad_w_value: float32 [2048, 1024], P(('dp', 'tm'), 'patch')
- grad_w_out: float32 [1024, 2048], P('patch', ('dp', 'tm'))
The draws below stay inside these ranges and needn't reach their ends.
All inputs are finite; a program needn't handle non-finite values.
Results may differ from the reference program's by a relative error of at most 0.035.
Values may be sent and summed in bfloat16 or wider, within the bound.
No kernel may reach another device: no remote copies, remote signals or barrier semaphores. Data moves between devices by JAX's collectives and lax.ppermute only.
A program may use at most 128 MiB of HBM per device.

```python
import math
import jax
import jax.numpy as jnp
from jax import lax

D = 2048
HEADS = 8
HS = 128
BATCH = 4
FRAMES = 16
PATCHES = 512
HD = 1024


def draw_inputs(key, part):
    key = jax.random.fold_in(key, 11)
    first, second, third = jax.random.split(key, 3)
    shape = (BATCH, FRAMES, PATCHES, D)
    row_scales = jnp.exp(jax.random.uniform(first, (BATCH, FRAMES, PATCHES, 1), jnp.float32, math.log(0.2), math.log(2.0)))
    column_scales = jnp.exp(jax.random.uniform(second, (1, 1, 1, D), jnp.float32, math.log(0.3), math.log(3.0)))
    base = jnp.clip(jax.random.normal(third, shape, jnp.float32), -4.0, 4.0)
    return (base * row_scales * column_scales).astype(jnp.bfloat16)


def shard_levels(rng, extent, shards, least, top_value):
    def one(position, parts):
        steps = jax.random.uniform(jax.random.fold_in(jax.random.fold_in(rng, 6), position), (parts,), jnp.float32, least / len(shards), top_value / len(shards))
        return jnp.repeat(jnp.exp(steps), extent[position] // parts).reshape((-1,) + (1,) * (len(extent) - position - 1))

    loudness = one(*shards[0])
    for cut in shards[1:]:
        loudness = loudness * one(*cut)
    return loudness


def bell_draw(key, shape, deviation, reach, shards=(), kind=jnp.bfloat16):
    drawn = jax.random.normal(key, shape, jnp.float32) * deviation
    if len(shards) > 0:
        drawn = shard_levels(key, shape, shards, -0.22, 0.18) * drawn
    return jnp.clip(drawn, min=-reach, max=reach).astype(kind)


def setup_inputs(seed: int = 0) -> dict:
    splits = jax.random.split(jax.random.key(seed), 7)
    return {
        "inputs": draw_inputs(jax.random.fold_in(splits[6], 71), 0),
        "w_query": bell_draw(splits[1], (D, HD), D ** -0.5, 0.125, ((1, 8),)),
        "w_key": bell_draw(splits[2], (D, HD), D ** -0.5, 0.125, ((1, 8),)),
        "w_value": bell_draw(splits[3], (D, HD), D ** -0.5, 0.125, ((1, 8),)),
        "w_out": bell_draw(splits[4], (HD, D), HD ** -0.5, 0.1875, ((0, 8),)),
        "grad_out": bell_draw(splits[5], (BATCH, FRAMES, PATCHES, D), 1.0, 6.0, ((0, 4), (1, 8), (2, 8))),
    }


highest = lax.Precision.HIGHEST
epsilon = 1e-06

def mix(form, left, right):
    return jnp.einsum(form, left.astype(jnp.float32), right.astype(jnp.float32), precision=highest)

def reference(inputs, w_query, w_key, w_value, w_out, grad_out):
    score_scale = 1.0 / math.sqrt(HS)
    head_shape = (BATCH, FRAMES, PATCHES, HEADS, HS)
    wide_x = inputs.astype(jnp.float32)
    inverse = lax.rsqrt(lax.optimization_barrier(jnp.mean(wide_x * wide_x, axis=-1, keepdims=True)) + epsilon)
    normed_wide = wide_x * inverse
    normed = normed_wide.astype(jnp.bfloat16)
    normed_flat = normed.reshape(-1, D)
    grad_flat = grad_out.reshape(-1, D)

    def project(weight):
        result = jnp.dot(normed_flat, weight, preferred_element_type=jnp.float32)
        return result.astype(jnp.bfloat16).reshape(head_shape)
    queries = project(w_query)
    keys_all = project(w_key)
    values_all = project(w_value)
    scores = mix('bfphs,bgphs->bphfg', queries, keys_all) * score_scale
    frame_ids = jnp.arange(FRAMES, dtype=jnp.int32)
    allowed = frame_ids[:, None] >= frame_ids[None, :]
    exped = jnp.where(allowed, jnp.exp(scores), jnp.zeros_like(scores))
    probs = exped / lax.optimization_barrier(jnp.sum(exped, axis=-1, keepdims=True))
    probs_low = probs.astype(jnp.bfloat16)
    mixed = mix('bphfg,bgphs->bfphs', probs_low, values_all).astype(jnp.bfloat16)
    grad_mixed = jnp.dot(grad_flat, w_out.T, preferred_element_type=jnp.float32)
    grad_mixed = grad_mixed.astype(jnp.bfloat16).reshape(head_shape)
    prob_grads = mix('bfphs,bgphs->bphfg', grad_mixed, values_all)
    delta = lax.optimization_barrier(jnp.sum(probs * prob_grads, axis=-1, keepdims=True))
    score_grads = (probs * (prob_grads - delta) * score_scale).astype(jnp.bfloat16)
    grad_queries = mix('bphfg,bgphs->bfphs', score_grads, keys_all).astype(jnp.bfloat16).reshape(-1, HD)
    grad_keys = mix('bphfg,bfphs->bgphs', score_grads, queries).astype(jnp.bfloat16).reshape(-1, HD)
    grad_values = mix('bphfg,bfphs->bgphs', probs_low, grad_mixed).astype(jnp.bfloat16).reshape(-1, HD)
    mixed_flat = mixed.reshape(-1, HD)
    grad_w_query = jnp.dot(normed_flat.T, grad_queries, preferred_element_type=jnp.float32)
    grad_w_key = jnp.dot(normed_flat.T, grad_keys, preferred_element_type=jnp.float32)
    grad_w_value = jnp.dot(normed_flat.T, grad_values, preferred_element_type=jnp.float32)
    grad_w_out = jnp.dot(mixed_flat.T, grad_flat, preferred_element_type=jnp.float32)
    grad_normed = jnp.dot(grad_queries, w_query.T, preferred_element_type=jnp.float32)
    grad_normed = grad_normed + jnp.dot(grad_keys, w_key.T, preferred_element_type=jnp.float32)
    grad_normed = grad_normed + jnp.dot(grad_values, w_value.T, preferred_element_type=jnp.float32)
    grad_normed = grad_normed.reshape(inputs.shape)
    mean_term = lax.optimization_barrier(jnp.mean(grad_normed * normed_wide, axis=-1, keepdims=True))
    grad_inputs = grad_out.astype(jnp.float32) + inverse * (grad_normed - normed_wide * mean_term)
    return (grad_inputs.astype(jnp.bfloat16), grad_w_query, grad_w_key, grad_w_value, grad_w_out)
```

```python
import math

import jax
import jax.numpy as jnp
from jax import lax
from jax.experimental import pallas as pl
from jax.experimental.pallas import tpu as pltpu
from jax.sharding import PartitionSpec as P

HS = 128
epsilon = 1e-06
f32 = jnp.float32
bf16 = jnp.bfloat16
PLANE = ("tm", "patch")


def plane_pairs(target):
    pairs = []
    for z in range(4):
        for core in range(2):
            for half in range(2):
                for x in range(4):
                    goal = target(z, core, half, x)
                    if goal is not None:
                        tz, tcore, thalf, tx = goal
                        pairs.append(
                            ((z * 2 + core) * 8 + half * 4 + x, (tz * 2 + tcore) * 8 + thalf * 4 + tx)
                        )
    return pairs


def to_core(array):
    return lax.ppermute(array, "tm", [(i, i ^ 1) for i in range(8)])


def to_x(array, step):
    return lax.ppermute(array, "patch", [(i, i ^ step) for i in range(8)])


def to_z(array, step):
    return lax.ppermute(array, "tm", [(i, i ^ (2 * step)) for i in range(8)])


def to_dp(array, step):
    return lax.ppermute(array, "dp", [(i, i ^ step) for i in range(4)])


def product(form, left, right):
    return jnp.einsum(form, left, right, preferred_element_type=f32)


def pick(array, index):
    return lax.dynamic_index_in_dim(array, index, 0, keepdims=False)


def attention_kernel(place, *refs):
    qkv_refs, cot_refs, out_refs = refs[:4], refs[4:8], refs[8:]
    scale = 1.0 / math.sqrt(HS)
    z, core = place[0], place[1]
    frames, columns = 16, qkv_refs[0].shape[1]
    rows = frames * columns
    qkv = jnp.concatenate([r[...] for r in qkv_refs], axis=0).reshape(rows, 3 * HS)
    cot = jnp.concatenate([r[...] for r in cot_refs], axis=0).reshape(rows, HS)
    queries, keys, values = qkv[:, :HS], qkv[:, HS : 2 * HS], qkv[:, 2 * HS :]

    def frame_of(index):
        slot = index // columns
        return ((slot // 4) ^ z) * 4 + (((slot % 4) // 2) ^ core) * 2 + slot % 2

    def dot(left, right, dims):
        return lax.dot_general(left, right, (dims, ((), ())), preferred_element_type=f32)

    row = lax.broadcasted_iota(jnp.int32, (rows, 1), 0)
    col = lax.broadcasted_iota(jnp.int32, (1, rows), 1)
    allowed = (row % columns == col % columns) & (frame_of(row) >= frame_of(col))
    scores = dot(queries, keys, ((1,), (1,))) * scale
    exped = jnp.where(allowed, jnp.exp(scores), 0.0)
    probs = exped / jnp.sum(exped, axis=-1, keepdims=True)
    prob_grads = dot(cot, values, ((1,), (1,)))
    delta = jnp.sum(probs * prob_grads, axis=-1, keepdims=True)
    score_grads = (probs * (prob_grads - delta) * scale).astype(bf16)
    probs_low = probs.astype(bf16)
    mixed = dot(probs_low, values, ((1,), (0,))).astype(bf16)
    grad_queries = dot(score_grads, keys, ((1,), (0,))).astype(bf16)
    grad_keys = dot(score_grads, queries, ((0,), (0,))).astype(bf16)
    grad_values = dot(probs_low, cot, ((0,), (0,))).astype(bf16)
    out = jnp.concatenate((grad_queries, grad_keys, grad_values, mixed), axis=-1)
    out = out.reshape(4, 4, columns, 4 * HS)
    for i in range(4):
        out_refs[i][...] = out[i]


def attention(place, qkv, cot):
    frames, patches, _ = qkv[0].shape
    block = 16
    spec = lambda width: pl.BlockSpec((frames, block, width), lambda i, _: (0, i, 0))
    return pl.pallas_call(
        attention_kernel,
        grid_spec=pltpu.PrefetchScalarGridSpec(
            num_scalar_prefetch=1,
            grid=(patches // block,),
            in_specs=[spec(3 * HS)] * 4 + [spec(HS)] * 4,
            out_specs=[spec(4 * HS)] * 4,
        ),
        out_shape=[jax.ShapeDtypeStruct((frames, patches, 4 * HS), bf16)] * 4,
        compiler_params=pltpu.CompilerParams(vmem_limit_bytes=32 * 2**20),
        cost_estimate=pl.CostEstimate(flops=500_000_000, bytes_accessed=2**21, transcendentals=2**18),
    )(place, *qkv, *cot)


def shards(inputs, w_query, w_key, w_value, w_out, grad_out):
    _, frames, patches, width = inputs.shape
    tokens = frames * patches
    tm, patch, dp = lax.axis_index("tm"), lax.axis_index("patch"), lax.axis_index("dp")
    z, core, half, x = tm // 2, tm % 2, patch // 4, patch % 4
    quarter = width // 4

    own_weights = jnp.concatenate((w_query, w_key, w_value, w_out.T), axis=1)
    keeps = core == half
    quarter_rows = lambda array, i: lax.dynamic_slice_in_dim(array, i * quarter, quarter, 0)
    part = lax.ppermute(
        quarter_rows(own_weights, dp),
        PLANE,
        plane_pairs(lambda z, core, half, x: (z, core, 1 - half, x) if core == half else None),
    )
    weights = own_weights
    for step in range(4):
        pairs = [
            ((d * 8 + t) * 8 + p, ((d ^ step) * 8 + t) * 8 + p)
            for d in range(4)
            for t in range(8)
            for p in range(8)
            if t % 2 != p // 4
        ]
        got = part if step == 0 else lax.ppermute(part, ("dp", "tm", "patch"), pairs)
        got = jnp.where(keeps, quarter_rows(own_weights, dp ^ step), got)
        weights = lax.dynamic_update_slice_in_dim(weights, got, (dp ^ step) * quarter, 0)

    wide_x = inputs.astype(f32)
    inverse = lax.rsqrt(jnp.mean(wide_x * wide_x, axis=-1, keepdims=True) + epsilon)
    normed_wide = wide_x * inverse
    normed = normed_wide.astype(bf16)

    def gather(array):
        array = array.reshape(tokens, width)
        mine = jnp.stack([array] + [to_x(array, step) for step in (1, 2, 3)])
        return jnp.stack((mine, to_core(mine)), axis=1)

    normed_all = gather(normed)
    cot_all = gather(grad_out)

    turn = z ^ x

    def scatter(array):
        pieces = [pick(array, turn ^ step).reshape(2 * frames, patches, -1) for step in range(4)]
        return [pieces[0]] + [to_z(pieces[step], step) for step in (1, 2, 3)]

    qkv = scatter(product("kctd,dh->kcth", normed_all, weights[:, : 3 * HS]).astype(bf16))
    cot = scatter(product("kctd,dh->kcth", cot_all, weights[:, 3 * HS :]).astype(bf16))
    place = jnp.stack((z, core)).astype(jnp.int32)
    grads = attention(place, qkv, cot)
    back = jnp.stack([grads[0]] + [to_z(grads[step], step) for step in (1, 2, 3)])
    back = jnp.stack([pick(back, turn ^ step) for step in range(4)])
    back = back.reshape(4, 2, tokens, 4 * HS)
    grad_qkv, mixed = back[..., : 3 * HS], back[..., 3 * HS :]

    partial = jnp.concatenate(
        (
            product("kctd,kcth->dh", normed_all, grad_qkv),
            product("kctd,kcth->dh", cot_all, mixed),
        ),
        axis=1,
    ).astype(bf16)
    partial = partial.reshape(4, quarter, 4 * HS)
    total = pick(partial, dp).astype(f32)
    for step in (1, 2, 3):
        total = total + to_dp(pick(partial, dp ^ step), step).astype(f32)
    partial = total.astype(bf16).reshape(4, quarter // 4, 4 * HS)
    total = pick(partial, z).astype(f32)
    for step in (1, 2, 3):
        total = total + to_z(pick(partial, z ^ step), step).astype(f32)
    partial = total.astype(bf16).reshape(2, quarter // 8, 4 * HS)
    first = lax.ppermute(
        pick(partial, half), PLANE, plane_pairs(lambda z, core, half, x: (z, half, core, x))
    )
    second = lax.ppermute(
        pick(partial, 1 - half), PLANE, plane_pairs(lambda z, core, half, x: (z, 1 - half, core, x))
    )
    reduced = first.astype(f32) + second.astype(f32)

    terms = product("kcth,dh->kctd", grad_qkv, weights[:, : 3 * HS])
    pair = terms[:, 0] + to_core(terms[:, 1].astype(bf16)).astype(f32)
    pair_low = pair.astype(bf16)
    grad_normed = pair[0]
    for step in (1, 2, 3):
        grad_normed = grad_normed + to_x(pair_low[step], step).astype(f32)
    grad_normed = grad_normed.reshape(inputs.shape)
    mean_term = jnp.mean(grad_normed * normed_wide, axis=-1, keepdims=True)
    grad_inputs = grad_out.astype(f32) + inverse * (grad_normed - normed_wide * mean_term)
    return (
        grad_inputs.astype(bf16),
        reduced[:, :HS],
        reduced[:, HS : 2 * HS],
        reduced[:, 2 * HS : 3 * HS],
        reduced[:, 3 * HS :].T,
    )


def solution(mesh):
    placed = (
        P("dp", "tm", "patch", None),
        P(None, "patch"),
        P(None, "patch"),
        P(None, "patch"),
        P("patch", None),
        P("dp", "tm", "patch", None),
    )
    return jax.shard_map(
        shards,
        mesh=mesh,
        in_specs=placed,
        out_specs=(
            P("dp", "tm", "patch", None),
            P(("dp", "tm"), "patch"),
            P(("dp", "tm"), "patch"),
            P(("dp", "tm"), "patch"),
            P("patch", ("dp", "tm")),
        ),
        check_vma=False,
    )
```

```python
import functools
import math

import jax
import jax.numpy as jnp
from jax import lax
from jax.experimental import pallas as pl
from jax.experimental.pallas import tpu as pltpu
from jax.sharding import PartitionSpec as P

HS = 128
epsilon = 1e-06
f32 = jnp.float32
bf16 = jnp.bfloat16
PLANE = ("tm", "patch")


def plane_pairs(target):
    pairs = []
    for z in range(4):
        for core in range(2):
            for half in range(2):
                for x in range(4):
                    goal = target(z, core, half, x)
                    if goal is not None:
                        tz, tcore, thalf, tx = goal
                        pairs.append(
                            ((z * 2 + core) * 8 + half * 4 + x, (tz * 2 + tcore) * 8 + thalf * 4 + tx)
                        )
    return pairs


def hop(array, axis, even, odd):
    if axis == "patch":
        pairs = plane_pairs(lambda z, core, half, x: (z, core, half, x ^ (odd if core else even)))
        return lax.ppermute(array, PLANE, pairs)
    pairs = [(d * 8 + t, (d ^ (odd if t % 2 else even)) * 8 + t) for d in range(4) for t in range(8)]
    return lax.ppermute(array, ("dp", "tm"), pairs)


def to_core(array):
    return lax.ppermute(array, "tm", [(i, i ^ 1) for i in range(8)])


def to_z(array, step):
    return lax.ppermute(array, "tm", [(i, i ^ (2 * step)) for i in range(8)])


def to_dp(array, step):
    return lax.ppermute(array, "dp", [(i, i ^ step) for i in range(4)])


def to_half(array):
    return lax.ppermute(array, "patch", [(i, i ^ 4) for i in range(8)])


def after(values, done):
    return lax.optimization_barrier((values, done))[0]


def pick(array, index):
    return lax.dynamic_index_in_dim(array, index, 0, keepdims=False)


def dot(left, right, left_dim, right_dim):
    dims = (((left_dim,), (right_dim,)), ((), ()))
    return lax.dot_general(left, right, dims, preferred_element_type=f32)


def array(shape, kind):
    return jax.ShapeDtypeStruct(shape, kind)


def call(kernel, out, inputs, place, grid, in_specs, out_specs, scratch=(), mib=16):
    return pl.pallas_call(
        kernel,
        grid_spec=pltpu.PrefetchScalarGridSpec(
            num_scalar_prefetch=1,
            grid=grid,
            in_specs=in_specs,
            out_specs=out_specs,
            scratch_shapes=scratch,
        ),
        out_shape=out,
        compiler_params=pltpu.CompilerParams(vmem_limit_bytes=mib * 2**20),
        cost_estimate=pl.CostEstimate(flops=1, bytes_accessed=1, transcendentals=0),
    )(place, *inputs)


def whole(shape):
    return pl.BlockSpec(shape, lambda i, p: (0,) * len(shape))


def attention_kernel(place, *refs):
    scale = 1.0 / math.sqrt(HS)
    z, core = place[0], place[1]
    in_refs, out_refs = refs[:4], refs[4:]
    frames, columns = 16, in_refs[0].shape[1]
    rows = frames * columns

    def frame_of(index):
        slot = index // columns
        return ((slot // 4) ^ z) * 4 + (((slot % 4) // 2) ^ core) * 2 + slot % 2

    row = lax.broadcasted_iota(jnp.int32, (rows, 1), 0)
    col = lax.broadcasted_iota(jnp.int32, (1, rows), 1)
    allowed = (row % columns == col % columns) & (frame_of(row) >= frame_of(col))
    packed = jnp.concatenate([r[...] for r in in_refs], axis=0).reshape(rows, 8 * HS)
    for head in range(2):
        qkv = packed[:, 3 * head * HS : 3 * (head + 1) * HS]
        queries, keys, values = qkv[:, :HS], qkv[:, HS : 2 * HS], qkv[:, 2 * HS :]
        cot = packed[:, (6 + head) * HS : (7 + head) * HS]
        scores = dot(queries, keys, 1, 1) * scale
        exped = jnp.where(allowed, jnp.exp(scores), 0.0)
        probs = exped / jnp.sum(exped, axis=-1, keepdims=True)
        prob_grads = dot(cot, values, 1, 1)
        delta = jnp.sum(probs * prob_grads, axis=-1, keepdims=True)
        score_grads = (probs * (prob_grads - delta) * scale).astype(bf16)
        probs_low = probs.astype(bf16)
        grads = (
            dot(score_grads, keys, 1, 0),
            dot(score_grads, queries, 0, 0),
            dot(probs_low, cot, 0, 0),
            dot(probs_low, values, 1, 0),
        )
        out = jnp.concatenate([g.astype(bf16) for g in grads], axis=-1)
        out = out.reshape(4, 4, columns, 4 * HS)
        for i in range(4):
            out_refs[i][:, :, 4 * head * HS : 4 * (head + 1) * HS] = out[i]


def attention(place, packed):
    frames, patches, _ = packed[0].shape
    block = 16
    spec = lambda width: pl.BlockSpec((frames, block, width), lambda i, p: (0, i, 0))
    return call(
        attention_kernel,
        [array((frames, patches, 8 * HS), bf16)] * 4,
        packed,
        place,
        (patches // block,),
        [spec(8 * HS)] * 4,
        [spec(8 * HS)] * 4,
    )


def flip_tokens_kernel(place, *refs):
    refs[-1][...] = jnp.concatenate([r[...] for r in refs[:-1]], axis=0).T


def flip_tokens(place, pieces):
    tokens, width = pieces[0].shape
    quarter = width // 4
    return call(
        flip_tokens_kernel,
        [array((width, 4 * tokens), bf16)],
        pieces,
        place,
        (4,),
        [pl.BlockSpec((tokens, quarter), lambda i, p: (0, i))] * 4,
        [pl.BlockSpec((quarter, 4 * tokens), lambda i, p: (i, 0))],
    )[0]


def rows_of(i, place):
    return (place[1] ^ (i // 2)) * 2 + ((place[2] // 2) ^ (i % 2))


def far_specs(quarter):
    return [
        pl.BlockSpec((quarter, 4 * HS), lambda i, p: (jnp.minimum(i, 1), 0)),
        pl.BlockSpec((quarter, 4 * HS), lambda i, p: (jnp.maximum(i - 2, 0), 0)),
    ]


def far_rows(place, refs):
    run = refs[0].shape[0] // 2
    odd = place[2] % 2
    parts = []
    for start in (odd, 1 - odd):
        rows = pl.ds(pl.multiple_of(start * run, run), run)
        parts.append(jnp.where(pl.program_id(0) < 2, refs[0][rows, :], refs[1][rows, :]))
    return jnp.concatenate(parts, axis=0)


def project_kernel(place, *refs):
    tokens, weights, (mine_ref, theirs_ref, total) = refs[:8], refs[8:14], refs[14:]
    i = pl.program_id(0)
    normed = jnp.concatenate([r[...] for r in tokens[:4]], axis=0)
    cot = jnp.concatenate([r[...] for r in tokens[4:]], axis=0)
    far = far_rows(place, weights[4:])
    wide = jnp.concatenate([r[...] for r in weights[:3]] + [far[:, : 3 * HS]], axis=1)
    parts = (
        dot(normed, wide, 1, 0),
        dot(cot, weights[3][...], 1, 1),
        dot(cot, far[:, 3 * HS :], 1, 0),
    )
    part = jnp.concatenate(parts, axis=1)

    @pl.when(i == 0)
    def _():
        total[...] = part

    @pl.when(i > 0)
    def _():
        total[...] += part

    @pl.when(i == 3)
    def _():
        steps, frames, half, columns = mine_ref.shape
        out = total[...].astype(bf16).reshape(steps, frames, 2, half, columns)
        core = place[1]
        mine_ref[...] = jnp.where(core == 0, out[:, :, 0], out[:, :, 1])
        theirs_ref[...] = jnp.where(core == 0, out[:, :, 1], out[:, :, 0])


def project(place, frames, normed, cot, weights):
    rows, width = normed[0].shape
    quarter = width // 4
    specs = [pl.BlockSpec((quarter, HS), lambda i, p: (rows_of(i, p), 0))] * 3
    specs = specs + [pl.BlockSpec((HS, quarter), lambda i, p: (0, rows_of(i, p)))]
    out = (4, frames, rows // frames // 2, 8 * HS)
    return call(
        project_kernel,
        [array(out, bf16)] * 2,
        (*normed, *cot, *weights),
        place,
        (4,),
        [pl.BlockSpec((rows, quarter), lambda i, p: (0, rows_of(i, p)))] * 8
        + specs
        + far_specs(quarter),
        [whole(out)] * 2,
        [pltpu.VMEM((4 * rows, 8 * HS), f32)],
        56,
    )


def order(core):
    return 2, 1 + 2 * core, 3 - 2 * core, 0


def in_order(i, core):
    first = jnp.where(i == 0, 2, 0)
    return jnp.where(i == 1, 1 + 2 * core, jnp.where(i == 2, 3 - 2 * core, first))


def join_patches(core, mine_ref, other_ref, out_ref):
    half = mine_ref.shape[2]
    out_ref[:, :, pl.ds(pl.multiple_of(core * half, half), half), :] = mine_ref[...]
    out_ref[:, :, pl.ds(pl.multiple_of((1 - core) * half, half), half), :] = other_ref[...]


def weight_kernel(place, normed, cot, mine_ref, other_ref, out_ref, grads_ref, *, keep):
    side = place[1] if keep else 1 - place[1]

    @pl.when(pl.program_id(0) == 0)
    def _():
        join_patches(place[1], mine_ref, other_ref, grads_ref)

    grads = grads_ref[...].reshape(-1, 8 * HS)
    wide = 3 * HS

    def rows(ref):
        both = ref[...].reshape(4, 2, -1, ref.shape[-1])
        return jnp.where(side == 0, both[:, 0], both[:, 1]).reshape(-1, ref.shape[-1])

    by_normed = jnp.concatenate((grads[:, :wide], grads[:, 4 * HS : 7 * HS]), axis=1)
    by_cot = jnp.concatenate((grads[:, wide : 4 * HS], grads[:, 7 * HS :]), axis=1)
    by_normed = dot(rows(normed), by_normed, 1, 0).astype(out_ref.dtype)
    by_cot = dot(rows(cot), by_cot, 1, 0).astype(out_ref.dtype)
    for head in range(2):
        start = 4 * head * HS
        out_ref[0, :, start : start + wide] = by_normed[:, head * wide : (head + 1) * wide]
        out_ref[0, :, start + wide : start + 4 * HS] = by_cot[:, head * HS : (head + 1) * HS]


def weight_grads(place, normed, cot, mine, other, keep):
    width, tokens = normed.shape
    quarter = width // 4
    tokens_spec = pl.BlockSpec(
        (quarter, tokens), lambda i, p: (p[2] ^ in_order(i, p[1] if keep else 1 - p[1]), 0)
    )
    shape = (4, quarter // 2, 8 * HS)
    return call(
        functools.partial(weight_kernel, keep=keep),
        [array(shape, f32 if keep else bf16)],
        (normed, cot, mine, other),
        place,
        (4,),
        [tokens_spec] * 2 + [whole(mine.shape)] * 2,
        [pl.BlockSpec((1, *shape[1:]), lambda i, p: (i, 0, 0))],
        [pltpu.VMEM(mine.shape[:2] + (2 * mine.shape[2], 8 * HS), bf16)],
    )[0]


def token_kernel(place, *refs):
    mine_ref, other_ref, weights, outs, (grads_ref, left_ref) = refs[0], refs[1], refs[2:7], refs[7:11], refs[11:]
    core = place[1]
    rows = outs[0].shape[0]

    @pl.when(pl.program_id(0) == 0)
    def _():
        join_patches(core, mine_ref, other_ref, grads_ref)
        for i, step in enumerate(order(core)):
            piece = grads_ref[step].reshape(rows, 8 * HS)
            piece = jnp.concatenate((piece[:, : 3 * HS], piece[:, 4 * HS : 7 * HS]), axis=1)
            left_ref[i * rows : (i + 1) * rows, :] = piece

    near = [r[...] for r in weights[:3]]
    right = jnp.concatenate(near + [far_rows(place, weights[3:])[:, : 3 * HS]], axis=1)
    out = dot(left_ref[...], right, 1, 1)
    for i, ref in enumerate(outs):
        ref[...] = out[i * rows : (i + 1) * rows].astype(ref.dtype)


def token_grads(place, grads, near, far):
    _, frames, half, _ = grads[0].shape
    rows, width = 2 * frames * half, near[0].shape[0]
    quarter = width // 4
    return call(
        token_kernel,
        [array((rows, width), kind) for kind in (bf16, bf16, f32, f32)],
        (*grads, *near, *far),
        place,
        (4,),
        [whole(grads[0].shape)] * 2
        + [pl.BlockSpec((quarter, HS), lambda i, p: (rows_of(i, p), 0))] * 3
        + far_specs(quarter),
        [pl.BlockSpec((rows, quarter), lambda i, p: (0, rows_of(i, p)))] * 4,
        [
            pltpu.VMEM((4, frames, 2 * half, 8 * HS), bf16),
            pltpu.VMEM((4 * rows, 6 * HS), bf16),
        ],
    )


def shards(inputs, w_query, w_key, w_value, w_out, grad_out):
    _, frames, patches, width = inputs.shape
    tokens = frames * patches
    tm, patch, dp = lax.axis_index("tm"), lax.axis_index("patch"), lax.axis_index("dp")
    z, core, half, x = tm // 2, tm % 2, patch // 4, patch % 4
    place = jnp.stack((z, core, dp)).astype(jnp.int32)
    even = core == 0
    eighth = width // 8

    def choose(first, second):
        return jnp.where(even, first, second)

    def ring_start(opposite, direct, axis):
        return hop(opposite.astype(bf16), axis, 1, 3), hop(direct.astype(bf16), axis, 1, 3)

    def ring_end(relayed, direct, late, own, axis):
        late = hop((late + relayed.astype(f32)).astype(bf16), axis, 3, 1)
        return own + direct.astype(f32) + late.astype(f32)

    cot = grad_out.reshape(tokens, width)
    cot_1, cot_3 = hop(cot, "patch", 1, 1), hop(cot, "patch", 3, 3)

    start = core * 4 * eighth + dp * eighth
    part = [lax.dynamic_slice_in_dim(w, start, eighth, 0) for w in (w_query, w_key, w_value)]
    part = part + [lax.dynamic_slice_in_dim(w_out, start, eighth, 1).T]
    part = jnp.concatenate(part, axis=1)
    inputs = after(inputs, part)
    part = to_half(part)

    wide_x = inputs.astype(f32)
    inverse = lax.rsqrt(jnp.mean(wide_x * wide_x, axis=-1, keepdims=True) + epsilon)
    normed_wide = wide_x * inverse
    normed = normed_wide.astype(bf16).reshape(tokens, width)

    normed_1, normed_3 = hop(normed, "patch", 1, 1), hop(normed, "patch", 3, 3)
    pieces = [part] + [to_dp(part, step) for step in (1, 2, 3)]
    cot_2 = after(choose(cot_3, cot_1), (pieces[1], pieces[3]))
    normed_2 = after(choose(normed_3, normed_1), (cot_2, pieces[2]))
    cot_2 = hop(cot_2, "patch", 1, 3)
    got = jnp.concatenate(after(pieces, (cot_2, normed_2)), axis=0)
    normed_2 = hop(normed_2, "patch", 1, 3)
    far = (got, to_core(got))
    normed_pieces = (normed, normed_1, normed_2, normed_3)
    turn = z ^ x

    def scatter(mine, theirs):
        both = jnp.stack((mine, to_core(theirs)), axis=1)
        shape = (2 * frames, patches // 2, mine.shape[-1])
        pieces = [pick(both, turn ^ step).reshape(shape) for step in range(4)]
        return [pieces[0]] + [to_z(pieces[step], step) for step in (1, 2, 3)]

    near = (w_query, w_key, w_value)
    cot_pieces = (cot, cot_1, cot_2, cot_3)
    weights = (*near, w_out, *far)
    packed = scatter(*project(place, frames, normed_pieces, cot_pieces, weights))
    normed_flat = flip_tokens(after(place, packed[1]), normed_pieces)
    cot_flat = flip_tokens(after(place, normed_flat), cot_pieces)
    grads = attention(after(place, cot_flat), packed)

    back = jnp.stack([grads[0]] + [to_z(grads[step], step) for step in (1, 2, 3)])
    back = jnp.stack([pick(back, turn ^ step) for step in range(4)])
    back = back.reshape(4, 2, frames, patches // 2, 8 * HS)
    back = (back[:, 0], to_core(back[:, 1]))

    given = weight_grads(place, normed_flat, cot_flat, *back, False)
    kept = weight_grads(after(place, given), normed_flat, cot_flat, *back, True)
    given = after(to_core(given), kept)
    pieces = [kept[i] + given[i].astype(f32) for i in range(4)]
    pieces = [piece.astype(bf16) for piece in pieces[:2]] + pieces[2:]
    weights_way = ring_start(*pieces[:2], "dp")
    terms = token_grads(after(place, pieces), back, near, far)
    tokens_way = ring_start(*terms[:2], "patch")
    relayed = after(weights_way[0], terms)
    partial = ring_end(relayed, weights_way[1], *pieces[2:], "dp").astype(bf16)
    tokens_way = (after(tokens_way[0], relayed), tokens_way[1])
    grad_normed = ring_end(*tokens_way, *terms[2:], "patch").reshape(inputs.shape)

    partial = partial.reshape(4, eighth // 4, 8 * HS)
    total = pick(partial, z).astype(f32)
    for step in (1, 2, 3):
        total = total + to_z(pick(partial, z ^ step), step).astype(f32)
    reduced = total[:, : 4 * HS] + to_half(total[:, 4 * HS :].astype(bf16)).astype(f32)

    mean_term = jnp.mean(grad_normed * normed_wide, axis=-1, keepdims=True)
    grad_inputs = grad_out.astype(f32) + inverse * (grad_normed - normed_wide * mean_term)
    return (
        grad_inputs.astype(bf16),
        reduced[:, :HS],
        reduced[:, HS : 2 * HS],
        reduced[:, 2 * HS : 3 * HS],
        reduced[:, 3 * HS :].T,
    )


def solution(mesh):
    placed = (
        P("dp", "tm", "patch", None),
        P(None, "patch"),
        P(None, "patch"),
        P(None, "patch"),
        P("patch", None),
        P("dp", "tm", "patch", None),
    )
    return jax.shard_map(
        shards,
        mesh=mesh,
        in_specs=placed,
        out_specs=(
            P("dp", "tm", "patch", None),
            P(("dp", "tm"), "patch"),
            P(("dp", "tm"), "patch"),
            P(("dp", "tm"), "patch"),
            P("patch", ("dp", "tm")),
        ),
        check_vma=False,
    )
```

```python
import functools
import math

import jax
import jax.numpy as jnp
from jax import lax
from jax.experimental import pallas as pl
from jax.experimental.pallas import tpu as pltpu
from jax.sharding import PartitionSpec as P

HS = 128
epsilon = 1e-06
f32 = jnp.float32
bf16 = jnp.bfloat16
PLANE = ("tm", "patch")


def plane_pairs(target):
    pairs = []
    for z in range(4):
        for core in range(2):
            for half in range(2):
                for x in range(4):
                    goal = target(z, core, half, x)
                    if goal is not None:
                        tz, tcore, thalf, tx = goal
                        pairs.append(
                            ((z * 2 + core) * 8 + half * 4 + x, (tz * 2 + tcore) * 8 + thalf * 4 + tx)
                        )
    return pairs


def hop(array, axis, even, odd):
    if axis == "patch":
        pairs = plane_pairs(lambda z, core, half, x: (z, core, half, x ^ (odd if core else even)))
        return lax.ppermute(array, PLANE, pairs)
    pairs = [(d * 8 + t, (d ^ (odd if t % 2 else even)) * 8 + t) for d in range(4) for t in range(8)]
    return lax.ppermute(array, ("dp", "tm"), pairs)


def to_core(array):
    return lax.ppermute(array, "tm", [(i, i ^ 1) for i in range(8)])


def to_z(array, step):
    return lax.ppermute(array, "tm", [(i, i ^ (2 * step)) for i in range(8)])


def to_dp(array, step):
    return lax.ppermute(array, "dp", [(i, i ^ step) for i in range(4)])


def to_half(array):
    return lax.ppermute(array, "patch", [(i, i ^ 4) for i in range(8)])


def after(values, done):
    return lax.optimization_barrier((values, done))[0]


def pick(array, index):
    return lax.dynamic_index_in_dim(array, index, 0, keepdims=False)


def dot(left, right, left_dim, right_dim):
    dims = (((left_dim,), (right_dim,)), ((), ()))
    return lax.dot_general(left, right, dims, preferred_element_type=f32)


def array(shape, kind):
    return jax.ShapeDtypeStruct(shape, kind)


def call(kernel, out, inputs, place, grid, in_specs, out_specs, scratch=(), mib=16):
    return pl.pallas_call(
        kernel,
        grid_spec=pltpu.PrefetchScalarGridSpec(
            num_scalar_prefetch=1,
            grid=grid,
            in_specs=in_specs,
            out_specs=out_specs,
            scratch_shapes=scratch,
        ),
        out_shape=out,
        compiler_params=pltpu.CompilerParams(vmem_limit_bytes=mib * 2**20),
        cost_estimate=pl.CostEstimate(flops=1, bytes_accessed=1, transcendentals=0),
    )(place, *inputs)


def whole(shape):
    return pl.BlockSpec(shape, lambda i, p: (0,) * len(shape))


def attention_kernel(place, *refs):
    scale = 1.0 / math.sqrt(HS)
    z, core = place[0], place[1]
    in_refs, out_refs = refs[:4], refs[4:]
    frames, columns = 16, in_refs[0].shape[1]
    rows = frames * columns

    def frame_of(index):
        slot = index // columns
        return ((slot // 4) ^ z) * 4 + (((slot % 4) // 2) ^ core) * 2 + slot % 2

    row = lax.broadcasted_iota(jnp.int32, (rows, 1), 0)
    col = lax.broadcasted_iota(jnp.int32, (1, rows), 1)
    allowed = (row % columns == col % columns) & (frame_of(row) >= frame_of(col))
    packed = jnp.concatenate([r[...] for r in in_refs], axis=0).reshape(rows, 8 * HS)
    for head in range(2):
        qkv = packed[:, 3 * head * HS : 3 * (head + 1) * HS]
        queries, keys, values = qkv[:, :HS], qkv[:, HS : 2 * HS], qkv[:, 2 * HS :]
        cot = packed[:, (6 + head) * HS : (7 + head) * HS]
        scores = dot(queries, keys, 1, 1) * scale
        exped = jnp.where(allowed, jnp.exp(scores), 0.0)
        probs = exped / jnp.sum(exped, axis=-1, keepdims=True)
        prob_grads = dot(cot, values, 1, 1)
        delta = jnp.sum(probs * prob_grads, axis=-1, keepdims=True)
        score_grads = (probs * (prob_grads - delta) * scale).astype(bf16)
        probs_low = probs.astype(bf16)
        grads = (
            dot(score_grads, keys, 1, 0),
            dot(score_grads, queries, 0, 0),
            dot(probs_low, cot, 0, 0),
            dot(probs_low, values, 1, 0),
        )
        out = jnp.concatenate([g.astype(bf16) for g in grads], axis=-1)
        out = out.reshape(4, 4, columns, 4 * HS)
        for i in range(4):
            out_refs[i][:, :, 4 * head * HS : 4 * (head + 1) * HS] = out[i]


def attention(place, packed):
    frames, patches, _ = packed[0].shape
    block = 16
    spec = lambda width: pl.BlockSpec((frames, block, width), lambda i, p: (0, i, 0))
    return call(
        attention_kernel,
        [array((frames, patches, 8 * HS), bf16)] * 4,
        packed,
        place,
        (patches // block,),
        [spec(8 * HS)] * 4,
        [spec(8 * HS)] * 4,
    )


def flip_tokens_kernel(place, *refs):
    refs[-1][...] = jnp.concatenate([r[...] for r in refs[:-1]], axis=0).T


def flip_tokens(place, pieces):
    tokens, width = pieces[0].shape
    quarter = width // 4
    return call(
        flip_tokens_kernel,
        [array((width, 4 * tokens), bf16)],
        pieces,
        place,
        (4,),
        [pl.BlockSpec((tokens, quarter), lambda i, p: (0, i))] * 4,
        [pl.BlockSpec((quarter, 4 * tokens), lambda i, p: (i, 0))],
    )[0]


def rows_of(i, place):
    return (place[1] ^ (i // 2)) * 2 + ((place[2] // 2) ^ (i % 2))


def far_specs(quarter):
    return [
        pl.BlockSpec((quarter, 4 * HS), lambda i, p: (jnp.minimum(i, 1), 0)),
        pl.BlockSpec((quarter, 4 * HS), lambda i, p: (jnp.maximum(i - 2, 0), 0)),
    ]


def far_rows(place, refs):
    run = refs[0].shape[0] // 2
    odd = place[2] % 2
    parts = []
    for start in (odd, 1 - odd):
        rows = pl.ds(pl.multiple_of(start * run, run), run)
        parts.append(jnp.where(pl.program_id(0) < 2, refs[0][rows, :], refs[1][rows, :]))
    return jnp.concatenate(parts, axis=0)


def project_kernel(place, *refs):
    tokens, weights, (mine_ref, theirs_ref, total) = refs[:8], refs[8:14], refs[14:]
    i = pl.program_id(0)
    normed = jnp.concatenate([r[...] for r in tokens[:4]], axis=0)
    cot = jnp.concatenate([r[...] for r in tokens[4:]], axis=0)
    far = far_rows(place, weights[4:])
    wide = jnp.concatenate([r[...] for r in weights[:3]] + [far[:, : 3 * HS]], axis=1)
    parts = (
        dot(normed, wide, 1, 0),
        dot(cot, weights[3][...], 1, 1),
        dot(cot, far[:, 3 * HS :], 1, 0),
    )
    part = jnp.concatenate(parts, axis=1)

    @pl.when(i == 0)
    def _():
        total[...] = part

    @pl.when(i > 0)
    def _():
        total[...] += part

    @pl.when(i == 3)
    def _():
        steps, frames, half, columns = mine_ref.shape
        out = total[...].astype(bf16).reshape(steps, frames, 2, half, columns)
        core = place[1]
        mine_ref[...] = jnp.where(core == 0, out[:, :, 0], out[:, :, 1])
        theirs_ref[...] = jnp.where(core == 0, out[:, :, 1], out[:, :, 0])


def project(place, frames, normed, cot, weights):
    rows, width = normed[0].shape
    quarter = width // 4
    specs = [pl.BlockSpec((quarter, HS), lambda i, p: (rows_of(i, p), 0))] * 3
    specs = specs + [pl.BlockSpec((HS, quarter), lambda i, p: (0, rows_of(i, p)))]
    out = (4, frames, rows // frames // 2, 8 * HS)
    return call(
        project_kernel,
        [array(out, bf16)] * 2,
        (*normed, *cot, *weights),
        place,
        (4,),
        [pl.BlockSpec((rows, quarter), lambda i, p: (0, rows_of(i, p)))] * 8
        + specs
        + far_specs(quarter),
        [whole(out)] * 2,
        [pltpu.VMEM((4 * rows, 8 * HS), f32)],
        56,
    )


def order(core):
    return 2, 1 + 2 * core, 3 - 2 * core, 0


def in_order(i, core):
    first = jnp.where(i == 0, 2, 0)
    return jnp.where(i == 1, 1 + 2 * core, jnp.where(i == 2, 3 - 2 * core, first))


def join_patches(core, mine_ref, other_ref, out_ref):
    half = mine_ref.shape[2]
    out_ref[:, :, pl.ds(pl.multiple_of(core * half, half), half), :] = mine_ref[...]
    out_ref[:, :, pl.ds(pl.multiple_of((1 - core) * half, half), half), :] = other_ref[...]


def weight_kernel(place, normed, cot, mine_ref, other_ref, out_ref, grads_ref, *, keep):
    side = place[1] if keep else 1 - place[1]

    @pl.when(pl.program_id(0) == 0)
    def _():
        join_patches(place[1], mine_ref, other_ref, grads_ref)

    grads = grads_ref[...].reshape(-1, 8 * HS)
    wide = 3 * HS

    def rows(ref):
        both = ref[...].reshape(4, 2, -1, ref.shape[-1])
        return jnp.where(side == 0, both[:, 0], both[:, 1]).reshape(-1, ref.shape[-1])

    by_normed = jnp.concatenate((grads[:, :wide], grads[:, 4 * HS : 7 * HS]), axis=1)
    by_cot = jnp.concatenate((grads[:, wide : 4 * HS], grads[:, 7 * HS :]), axis=1)
    by_normed = dot(rows(normed), by_normed, 1, 0).astype(out_ref.dtype)
    by_cot = dot(rows(cot), by_cot, 1, 0).astype(out_ref.dtype)
    for head in range(2):
        start = 4 * head * HS
        out_ref[0, :, start : start + wide] = by_normed[:, head * wide : (head + 1) * wide]
        out_ref[0, :, start + wide : start + 4 * HS] = by_cot[:, head * HS : (head + 1) * HS]


def weight_grads(place, normed, cot, mine, other, keep):
    width, tokens = normed.shape
    quarter = width // 4
    tokens_spec = pl.BlockSpec(
        (quarter, tokens), lambda i, p: (p[2] ^ in_order(i, p[1] if keep else 1 - p[1]), 0)
    )
    shape = (4, quarter // 2, 8 * HS)
    return call(
        functools.partial(weight_kernel, keep=keep),
        [array(shape, f32 if keep else bf16)],
        (normed, cot, mine, other),
        place,
        (4,),
        [tokens_spec] * 2 + [whole(mine.shape)] * 2,
        [pl.BlockSpec((1, *shape[1:]), lambda i, p: (i, 0, 0))],
        [pltpu.VMEM(mine.shape[:2] + (2 * mine.shape[2], 8 * HS), bf16)],
    )[0]


def token_kernel(place, *refs):
    mine_ref, other_ref, weights, outs, (grads_ref, left_ref) = refs[0], refs[1], refs[2:7], refs[7:11], refs[11:]
    core = place[1]
    rows = outs[0].shape[0]

    @pl.when(pl.program_id(0) == 0)
    def _():
        join_patches(core, mine_ref, other_ref, grads_ref)
        for i, step in enumerate(order(core)):
            piece = grads_ref[step].reshape(rows, 8 * HS)
            piece = jnp.concatenate((piece[:, : 3 * HS], piece[:, 4 * HS : 7 * HS]), axis=1)
            left_ref[i * rows : (i + 1) * rows, :] = piece

    near = [r[...] for r in weights[:3]]
    right = jnp.concatenate(near + [far_rows(place, weights[3:])[:, : 3 * HS]], axis=1)
    out = dot(left_ref[...], right, 1, 1)
    for i, ref in enumerate(outs):
        ref[...] = out[i * rows : (i + 1) * rows].astype(ref.dtype)


def token_grads(place, grads, near, far):
    _, frames, half, _ = grads[0].shape
    rows, width = 2 * frames * half, near[0].shape[0]
    quarter = width // 4
    return call(
        token_kernel,
        [array((rows, width), kind) for kind in (bf16, bf16, f32, f32)],
        (*grads, *near, *far),
        place,
        (4,),
        [whole(grads[0].shape)] * 2
        + [pl.BlockSpec((quarter, HS), lambda i, p: (rows_of(i, p), 0))] * 3
        + far_specs(quarter),
        [pl.BlockSpec((rows, quarter), lambda i, p: (0, rows_of(i, p)))] * 4,
        [
            pltpu.VMEM((4, frames, 2 * half, 8 * HS), bf16),
            pltpu.VMEM((4 * rows, 6 * HS), bf16),
        ],
    )


def shards(inputs, w_query, w_key, w_value, w_out, grad_out):
    _, frames, patches, width = inputs.shape
    tokens = frames * patches
    tm, patch, dp = lax.axis_index("tm"), lax.axis_index("patch"), lax.axis_index("dp")
    z, core, half, x = tm // 2, tm % 2, patch // 4, patch % 4
    place = jnp.stack((z, core, dp)).astype(jnp.int32)
    even = core == 0
    eighth = width // 8

    def choose(first, second):
        return jnp.where(even, first, second)

    def ring_start(opposite, direct, axis):
        return hop(opposite.astype(bf16), axis, 1, 3), hop(direct.astype(bf16), axis, 1, 3)

    def ring_end(relayed, direct, late, own, axis):
        late = hop((late + relayed.astype(f32)).astype(bf16), axis, 3, 1)
        return own + direct.astype(f32) + late.astype(f32)

    cot = grad_out.reshape(tokens, width)
    cot_1, cot_3 = hop(cot, "patch", 1, 1), hop(cot, "patch", 3, 3)

    start = core * 4 * eighth + dp * eighth
    part = [lax.dynamic_slice_in_dim(w, start, eighth, 0) for w in (w_query, w_key, w_value)]
    part = part + [lax.dynamic_slice_in_dim(w_out, start, eighth, 1).T]
    part = jnp.concatenate(part, axis=1)
    inputs = after(inputs, part)
    part = to_half(part)

    wide_x = inputs.astype(f32)
    inverse = lax.rsqrt(jnp.mean(wide_x * wide_x, axis=-1, keepdims=True) + epsilon)
    normed_wide = wide_x * inverse
    normed = normed_wide.astype(bf16).reshape(tokens, width)

    normed_1, normed_3 = hop(normed, "patch", 1, 1), hop(normed, "patch", 3, 3)
    pieces = [part] + [to_dp(part, step) for step in (1, 2, 3)]
    cot_2 = after(choose(cot_3, cot_1), (pieces[1], pieces[3]))
    normed_2 = after(choose(normed_3, normed_1), cot_2)
    cot_2, normed_2 = hop(cot_2, "patch", 1, 3), hop(normed_2, "patch", 1, 3)
    got = jnp.concatenate(after(pieces, (cot_2, normed_2)), axis=0)
    far = (got, to_core(got))
    normed_pieces = (normed, normed_1, normed_2, normed_3)
    turn = z ^ x

    def scatter(mine, theirs):
        both = jnp.stack((mine, to_core(theirs)), axis=1)
        shape = (2 * frames, patches // 2, mine.shape[-1])
        pieces = [pick(both, turn ^ step).reshape(shape) for step in range(4)]
        return [pieces[0]] + [to_z(pieces[step], step) for step in (1, 2, 3)]

    near = (w_query, w_key, w_value)
    cot_pieces = (cot, cot_1, cot_2, cot_3)
    weights = (*near, w_out, *far)
    packed = scatter(*project(place, frames, normed_pieces, cot_pieces, weights))
    normed_flat = flip_tokens(after(place, packed[1]), normed_pieces)
    cot_flat = flip_tokens(after(place, normed_flat), cot_pieces)
    grads = attention(after(place, cot_flat), packed)

    back = jnp.stack([grads[0]] + [to_z(grads[step], step) for step in (1, 2, 3)])
    back = jnp.stack([pick(back, turn ^ step) for step in range(4)])
    back = back.reshape(4, 2, frames, patches // 2, 8 * HS)
    back = (back[:, 0], to_core(back[:, 1]))

    given = weight_grads(place, normed_flat, cot_flat, *back, False)
    kept = weight_grads(after(place, given), normed_flat, cot_flat, *back, True)
    given = after(to_core(given), kept)
    pieces = [kept[i] + given[i].astype(f32) for i in range(4)]
    pieces = [piece.astype(bf16) for piece in pieces[:2]] + pieces[2:]
    weights_way = ring_start(*pieces[:2], "dp")
    terms = token_grads(after(place, pieces), back, near, far)
    tokens_way = ring_start(*terms[:2], "patch")
    relayed = after(weights_way[0], terms)
    partial = ring_end(relayed, weights_way[1], *pieces[2:], "dp").astype(bf16)
    tokens_way = (after(tokens_way[0], relayed), tokens_way[1])
    grad_normed = ring_end(*tokens_way, *terms[2:], "patch").reshape(inputs.shape)

    partial = partial.reshape(4, eighth // 4, 8 * HS)
    total = pick(partial, z).astype(f32)
    for step in (1, 2, 3):
        total = total + to_z(pick(partial, z ^ step), step).astype(f32)
    reduced = total[:, : 4 * HS] + to_half(total[:, 4 * HS :].astype(bf16)).astype(f32)

    mean_term = jnp.mean(grad_normed * normed_wide, axis=-1, keepdims=True)
    grad_inputs = grad_out.astype(f32) + inverse * (grad_normed - normed_wide * mean_term)
    return (
        grad_inputs.astype(bf16),
        reduced[:, :HS],
        reduced[:, HS : 2 * HS],
        reduced[:, 2 * HS : 3 * HS],
        reduced[:, 3 * HS :].T,
    )


def solution(mesh):
    placed = (
        P("dp", "tm", "patch", None),
        P(None, "patch"),
        P(None, "patch"),
        P(None, "patch"),
        P("patch", None),
        P("dp", "tm", "patch", None),
    )
    return jax.shard_map(
        shards,
        mesh=mesh,
        in_specs=placed,
        out_specs=(
            P("dp", "tm", "patch", None),
            P(("dp", "tm"), "patch"),
            P(("dp", "tm"), "patch"),
            P(("dp", "tm"), "patch"),
            P("patch", ("dp", "tm")),
        ),
        check_vma=False,
    )
```

```python
import functools
import math

import jax
import jax.numpy as jnp
from jax import lax
from jax.experimental import pallas as pl
from jax.experimental.pallas import tpu as pltpu
from jax.sharding import PartitionSpec as P

HS = 128
epsilon = 1e-06
f32 = jnp.float32
bf16 = jnp.bfloat16
PLANE = ("tm", "patch")


def plane_pairs(target):
    pairs = []
    for z in range(4):
        for core in range(2):
            for half in range(2):
                for x in range(4):
                    goal = target(z, core, half, x)
                    if goal is not None:
                        tz, tcore, thalf, tx = goal
                        pairs.append(
                            ((z * 2 + core) * 8 + half * 4 + x, (tz * 2 + tcore) * 8 + thalf * 4 + tx)
                        )
    return pairs


def hop(array, axis, even, odd):
    if axis == "patch":
        pairs = plane_pairs(lambda z, core, half, x: (z, core, half, x ^ (odd if core else even)))
        return lax.ppermute(array, PLANE, pairs)
    pairs = [(d * 8 + t, (d ^ (odd if t % 2 else even)) * 8 + t) for d in range(4) for t in range(8)]
    return lax.ppermute(array, ("dp", "tm"), pairs)


def to_core(array):
    return lax.ppermute(array, "tm", [(i, i ^ 1) for i in range(8)])


def to_z(array, step):
    return lax.ppermute(array, "tm", [(i, i ^ (2 * step)) for i in range(8)])


def to_dp(array, step):
    return lax.ppermute(array, "dp", [(i, i ^ step) for i in range(4)])


def to_half(array):
    return lax.ppermute(array, "patch", [(i, i ^ 4) for i in range(8)])


def after(values, done):
    return lax.optimization_barrier((values, done))[0]


def pick(array, index):
    return lax.dynamic_index_in_dim(array, index, 0, keepdims=False)


def dot(left, right, left_dim, right_dim):
    dims = (((left_dim,), (right_dim,)), ((), ()))
    return lax.dot_general(left, right, dims, preferred_element_type=f32)


def array(shape, kind):
    return jax.ShapeDtypeStruct(shape, kind)


def call(kernel, out, inputs, place, grid, in_specs, out_specs, scratch=(), mib=16):
    return pl.pallas_call(
        kernel,
        grid_spec=pltpu.PrefetchScalarGridSpec(
            num_scalar_prefetch=1,
            grid=grid,
            in_specs=in_specs,
            out_specs=out_specs,
            scratch_shapes=scratch,
        ),
        out_shape=out,
        compiler_params=pltpu.CompilerParams(vmem_limit_bytes=mib * 2**20),
        cost_estimate=pl.CostEstimate(flops=1, bytes_accessed=1, transcendentals=0),
    )(place, *inputs)


def whole(shape):
    return pl.BlockSpec(shape, lambda i, p: (0,) * len(shape))


def attention_kernel(place, *refs):
    scale = 1.0 / math.sqrt(HS)
    z, core = place[0], place[1]
    in_refs, out_refs = refs[:4], refs[4:]
    frames, columns = 16, in_refs[0].shape[1]
    rows = frames * columns

    def frame_of(index):
        slot = index // columns
        return ((slot // 4) ^ z) * 4 + (((slot % 4) // 2) ^ core) * 2 + slot % 2

    row = lax.broadcasted_iota(jnp.int32, (rows, 1), 0)
    col = lax.broadcasted_iota(jnp.int32, (1, rows), 1)
    allowed = (row % columns == col % columns) & (frame_of(row) >= frame_of(col))
    packed = jnp.concatenate([r[...] for r in in_refs], axis=0).reshape(rows, 8 * HS)
    for head in range(2):
        qkv = packed[:, 3 * head * HS : 3 * (head + 1) * HS]
        queries, keys, values = qkv[:, :HS], qkv[:, HS : 2 * HS], qkv[:, 2 * HS :]
        cot = packed[:, (6 + head) * HS : (7 + head) * HS]
        scores = dot(queries, keys, 1, 1) * scale
        exped = jnp.where(allowed, jnp.exp(scores), 0.0)
        probs = exped / jnp.sum(exped, axis=-1, keepdims=True)
        prob_grads = dot(cot, values, 1, 1)
        delta = jnp.sum(probs * prob_grads, axis=-1, keepdims=True)
        score_grads = (probs * (prob_grads - delta) * scale).astype(bf16)
        probs_low = probs.astype(bf16)
        grads = (
            dot(score_grads, keys, 1, 0),
            dot(score_grads, queries, 0, 0),
            dot(probs_low, cot, 0, 0),
            dot(probs_low, values, 1, 0),
        )
        out = jnp.concatenate([g.astype(bf16) for g in grads], axis=-1)
        out = out.reshape(4, 4, columns, 4 * HS)
        for i in range(4):
            out_refs[i][:, :, 4 * head * HS : 4 * (head + 1) * HS] = out[i]


def attention(place, packed):
    frames, patches, _ = packed[0].shape
    block = 16
    spec = lambda width: pl.BlockSpec((frames, block, width), lambda i, p: (0, i, 0))
    return call(
        attention_kernel,
        [array((frames, patches, 8 * HS), bf16)] * 4,
        packed,
        place,
        (patches // block,),
        [spec(8 * HS)] * 4,
        [spec(8 * HS)] * 4,
    )


def flip_tokens_kernel(place, *refs):
    refs[-1][...] = jnp.concatenate([r[...] for r in refs[:-1]], axis=0).T


def flip_tokens(place, pieces):
    tokens, width = pieces[0].shape
    quarter = width // 4
    return call(
        flip_tokens_kernel,
        [array((width, 4 * tokens), bf16)],
        pieces,
        place,
        (4,),
        [pl.BlockSpec((tokens, quarter), lambda i, p: (0, i))] * 4,
        [pl.BlockSpec((quarter, 4 * tokens), lambda i, p: (i, 0))],
    )[0]


def rows_of(i, place):
    return (place[1] ^ (i // 2)) * 2 + ((place[2] // 2) ^ (i % 2))


def far_specs(quarter):
    return [
        pl.BlockSpec((quarter, 4 * HS), lambda i, p: (jnp.minimum(i, 1), 0)),
        pl.BlockSpec((quarter, 4 * HS), lambda i, p: (jnp.maximum(i - 2, 0), 0)),
    ]


def far_rows(place, refs):
    run = refs[0].shape[0] // 2
    odd = place[2] % 2
    parts = []
    for start in (odd, 1 - odd):
        rows = pl.ds(pl.multiple_of(start * run, run), run)
        parts.append(jnp.where(pl.program_id(0) < 2, refs[0][rows, :], refs[1][rows, :]))
    return jnp.concatenate(parts, axis=0)


def project_kernel(place, *refs):
    tokens, weights, (mine_ref, theirs_ref, total) = refs[:8], refs[8:14], refs[14:]
    i = pl.program_id(0)
    normed = jnp.concatenate([r[...] for r in tokens[:4]], axis=0)
    cot = jnp.concatenate([r[...] for r in tokens[4:]], axis=0)
    far = far_rows(place, weights[4:])
    wide = jnp.concatenate([r[...] for r in weights[:3]] + [far[:, : 3 * HS]], axis=1)
    narrow = jnp.concatenate((weights[3][...].T, far[:, 3 * HS :]), axis=1)
    part = jnp.concatenate((dot(normed, wide, 1, 0), dot(cot, narrow, 1, 0)), axis=1)

    @pl.when(i == 0)
    def _():
        total[...] = part

    @pl.when(i > 0)
    def _():
        total[...] += part

    @pl.when(i == 3)
    def _():
        steps, frames, half, columns = mine_ref.shape
        out = total[...].astype(bf16).reshape(steps, frames, 2, half, columns)
        core = place[1]
        mine_ref[...] = jnp.where(core == 0, out[:, :, 0], out[:, :, 1])
        theirs_ref[...] = jnp.where(core == 0, out[:, :, 1], out[:, :, 0])


def project(place, frames, normed, cot, weights):
    rows, width = normed[0].shape
    quarter = width // 4
    specs = [pl.BlockSpec((quarter, HS), lambda i, p: (rows_of(i, p), 0))] * 3
    specs = specs + [pl.BlockSpec((HS, quarter), lambda i, p: (0, rows_of(i, p)))]
    out = (4, frames, rows // frames // 2, 8 * HS)
    return call(
        project_kernel,
        [array(out, bf16)] * 2,
        (*normed, *cot, *weights),
        place,
        (4,),
        [pl.BlockSpec((rows, quarter), lambda i, p: (0, rows_of(i, p)))] * 8
        + specs
        + far_specs(quarter),
        [whole(out)] * 2,
        [pltpu.VMEM((4 * rows, 8 * HS), f32)],
        56,
    )


def order(core):
    return 2, 1 + 2 * core, 3 - 2 * core, 0


def in_order(i, core):
    first = jnp.where(i == 0, 2, 0)
    return jnp.where(i == 1, 1 + 2 * core, jnp.where(i == 2, 3 - 2 * core, first))


def join_patches(core, mine_ref, other_ref, out_ref):
    half = mine_ref.shape[2]
    out_ref[:, :, pl.ds(pl.multiple_of(core * half, half), half), :] = mine_ref[...]
    out_ref[:, :, pl.ds(pl.multiple_of((1 - core) * half, half), half), :] = other_ref[...]


def weight_kernel(place, normed, cot, mine_ref, other_ref, out_ref, grads_ref, *, keep):
    side = place[1] if keep else 1 - place[1]

    @pl.when(pl.program_id(0) == 0)
    def _():
        join_patches(place[1], mine_ref, other_ref, grads_ref)

    grads = grads_ref[...].reshape(-1, 8 * HS)
    wide = 3 * HS

    def rows(ref):
        both = ref[...].reshape(4, 2, -1, ref.shape[-1])
        return jnp.where(side == 0, both[:, 0], both[:, 1]).reshape(-1, ref.shape[-1])

    by_normed = jnp.concatenate((grads[:, :wide], grads[:, 4 * HS : 7 * HS]), axis=1)
    by_cot = jnp.concatenate((grads[:, wide : 4 * HS], grads[:, 7 * HS :]), axis=1)
    by_normed = dot(rows(normed), by_normed, 1, 0).astype(out_ref.dtype)
    by_cot = dot(rows(cot), by_cot, 1, 0).astype(out_ref.dtype)
    for head in range(2):
        start = 4 * head * HS
        out_ref[0, :, start : start + wide] = by_normed[:, head * wide : (head + 1) * wide]
        out_ref[0, :, start + wide : start + 4 * HS] = by_cot[:, head * HS : (head + 1) * HS]


def weight_grads(place, normed, cot, mine, other, keep):
    width, tokens = normed.shape
    quarter = width // 4
    tokens_spec = pl.BlockSpec(
        (quarter, tokens), lambda i, p: (p[2] ^ in_order(i, p[1] if keep else 1 - p[1]), 0)
    )
    shape = (4, quarter // 2, 8 * HS)
    return call(
        functools.partial(weight_kernel, keep=keep),
        [array(shape, f32 if keep else bf16)],
        (normed, cot, mine, other),
        place,
        (4,),
        [tokens_spec] * 2 + [whole(mine.shape)] * 2,
        [pl.BlockSpec((1, *shape[1:]), lambda i, p: (i, 0, 0))],
        [pltpu.VMEM(mine.shape[:2] + (2 * mine.shape[2], 8 * HS), bf16)],
    )[0]


def token_kernel(place, *refs):
    mine_ref, other_ref, weights, outs, (grads_ref, left_ref) = refs[0], refs[1], refs[2:7], refs[7:11], refs[11:]
    core = place[1]
    rows = outs[0].shape[0]

    @pl.when(pl.program_id(0) == 0)
    def _():
        join_patches(core, mine_ref, other_ref, grads_ref)
        for i, step in enumerate(order(core)):
            piece = grads_ref[step].reshape(rows, 8 * HS)
            piece = jnp.concatenate((piece[:, : 3 * HS], piece[:, 4 * HS : 7 * HS]), axis=1)
            left_ref[i * rows : (i + 1) * rows, :] = piece

    near = [r[...] for r in weights[:3]]
    right = jnp.concatenate(near + [far_rows(place, weights[3:])[:, : 3 * HS]], axis=1)
    out = dot(left_ref[...], right.T, 1, 0)
    for i, ref in enumerate(outs):
        ref[...] = out[i * rows : (i + 1) * rows].astype(ref.dtype)


def token_grads(place, grads, near, far):
    _, frames, half, _ = grads[0].shape
    rows, width = 2 * frames * half, near[0].shape[0]
    quarter = width // 4
    return call(
        token_kernel,
        [array((rows, width), kind) for kind in (bf16, bf16, f32, f32)],
        (*grads, *near, *far),
        place,
        (4,),
        [whole(grads[0].shape)] * 2
        + [pl.BlockSpec((quarter, HS), lambda i, p: (rows_of(i, p), 0))] * 3
        + far_specs(quarter),
        [pl.BlockSpec((rows, quarter), lambda i, p: (0, rows_of(i, p)))] * 4,
        [
            pltpu.VMEM((4, frames, 2 * half, 8 * HS), bf16),
            pltpu.VMEM((4 * rows, 6 * HS), bf16),
        ],
    )


def shards(inputs, w_query, w_key, w_value, w_out, grad_out):
    _, frames, patches, width = inputs.shape
    tokens = frames * patches
    tm, patch, dp = lax.axis_index("tm"), lax.axis_index("patch"), lax.axis_index("dp")
    z, core, half, x = tm // 2, tm % 2, patch // 4, patch % 4
    place = jnp.stack((z, core, dp)).astype(jnp.int32)
    even = core == 0
    eighth = width // 8

    def choose(first, second):
        return jnp.where(even, first, second)

    def ring_start(opposite, direct, axis):
        return hop(opposite.astype(bf16), axis, 1, 3), hop(direct.astype(bf16), axis, 1, 3)

    def ring_end(relayed, direct, late, own, axis):
        late = hop((late + relayed.astype(f32)).astype(bf16), axis, 3, 1)
        return own + direct.astype(f32) + late.astype(f32)

    cot = grad_out.reshape(tokens, width)
    cot_1, cot_3 = hop(cot, "patch", 1, 1), hop(cot, "patch", 3, 3)

    start = core * 4 * eighth + dp * eighth
    part = [lax.dynamic_slice_in_dim(w, start, eighth, 0) for w in (w_query, w_key, w_value)]
    part = part + [lax.dynamic_slice_in_dim(w_out, start, eighth, 1).T]
    part = jnp.concatenate(part, axis=1)
    inputs = after(inputs, (part, place))
    part = to_half(part)

    wide_x = inputs.astype(f32)
    inverse = lax.rsqrt(jnp.mean(wide_x * wide_x, axis=-1, keepdims=True) + epsilon)
    normed_wide = wide_x * inverse
    normed = normed_wide.astype(bf16).reshape(tokens, width)

    normed_1, normed_3 = hop(normed, "patch", 1, 1), hop(normed, "patch", 3, 3)
    pieces = [part] + [to_dp(part, step) for step in (1, 2, 3)]
    cot_2 = after(choose(cot_3, cot_1), (pieces[1], pieces[3]))
    normed_2 = after(choose(normed_3, normed_1), cot_2)
    cot_2, normed_2 = hop(cot_2, "patch", 1, 3), hop(normed_2, "patch", 1, 3)
    got = jnp.concatenate(after(pieces, (cot_2, normed_2)), axis=0)
    far = (got, to_core(got))
    normed_pieces = (normed, normed_1, normed_2, normed_3)
    turn = z ^ x

    def scatter(mine, theirs):
        both = jnp.stack((mine, to_core(theirs)), axis=1)
        shape = (2 * frames, patches // 2, mine.shape[-1])
        pieces = [pick(both, turn ^ step).reshape(shape) for step in range(4)]
        return [pieces[0]] + [to_z(pieces[step], step) for step in (1, 2, 3)]

    near = (w_query, w_key, w_value)
    cot_pieces = (cot, cot_1, cot_2, cot_3)
    weights = (*near, w_out, *far)
    packed = scatter(*project(place, frames, normed_pieces, cot_pieces, weights))
    normed_flat = flip_tokens(after(place, packed[1]), normed_pieces)
    cot_flat = flip_tokens(after(place, normed_flat), cot_pieces)
    grads = attention(after(place, cot_flat), packed)

    back = jnp.stack([grads[0]] + [to_z(grads[step], step) for step in (1, 2, 3)])
    back = jnp.stack([pick(back, turn ^ step) for step in range(4)])
    back = back.reshape(4, 2, frames, patches // 2, 8 * HS)
    back = (back[:, 0], to_core(back[:, 1]))

    given = weight_grads(place, normed_flat, cot_flat, *back, False)
    kept = weight_grads(after(place, given), normed_flat, cot_flat, *back, True)
    given = after(to_core(given), kept)
    pieces = [kept[i] + given[i].astype(f32) for i in range(4)]
    pieces = [piece.astype(bf16) for piece in pieces[:2]] + pieces[2:]
    weights_way = ring_start(*pieces[:2], "dp")
    terms = token_grads(after(place, pieces), back, near, far)
    tokens_way = ring_start(*terms[:2], "patch")
    relayed = after(weights_way[0], terms)
    partial = ring_end(relayed, weights_way[1], *pieces[2:], "dp").astype(bf16)
    tokens_way = (after(tokens_way[0], relayed), tokens_way[1])
    grad_normed = ring_end(*tokens_way, *terms[2:], "patch").reshape(inputs.shape)

    partial = partial.reshape(4, eighth // 4, 8 * HS)
    total = pick(partial, z).astype(f32)
    for step in (1, 2, 3):
        total = total + to_z(pick(partial, z ^ step), step).astype(f32)
    reduced = total[:, : 4 * HS] + to_half(total[:, 4 * HS :].astype(bf16)).astype(f32)

    mean_term = jnp.mean(grad_normed * normed_wide, axis=-1, keepdims=True)
    grad_inputs = grad_out.astype(f32) + inverse * (grad_normed - normed_wide * mean_term)
    return (
        grad_inputs.astype(bf16),
        reduced[:, :HS],
        reduced[:, HS : 2 * HS],
        reduced[:, 2 * HS : 3 * HS],
        reduced[:, 3 * HS :].T,
    )


def solution(mesh):
    placed = (
        P("dp", "tm", "patch", None),
        P(None, "patch"),
        P(None, "patch"),
        P(None, "patch"),
        P("patch", None),
        P("dp", "tm", "patch", None),
    )
    return jax.shard_map(
        shards,
        mesh=mesh,
        in_specs=placed,
        out_specs=(
            P("dp", "tm", "patch", None),
            P(("dp", "tm"), "patch"),
            P(("dp", "tm"), "patch"),
            P(("dp", "tm"), "patch"),
            P("patch", ("dp", "tm")),
        ),
        check_vma=False,
    )
```

```python
import functools
import math

import jax
import jax.numpy as jnp
from jax import lax
from jax.experimental import pallas as pl
from jax.experimental.pallas import tpu as pltpu
from jax.sharding import PartitionSpec as P

HS = 128
epsilon = 1e-06
f32 = jnp.float32
bf16 = jnp.bfloat16
PLANE = ("tm", "patch")


def plane_pairs(target):
    pairs = []
    for z in range(4):
        for core in range(2):
            for half in range(2):
                for x in range(4):
                    goal = target(z, core, half, x)
                    if goal is not None:
                        tz, tcore, thalf, tx = goal
                        pairs.append(
                            ((z * 2 + core) * 8 + half * 4 + x, (tz * 2 + tcore) * 8 + thalf * 4 + tx)
                        )
    return pairs


def hop(array, axis, even, odd):
    if axis == "patch":
        pairs = plane_pairs(lambda z, core, half, x: (z, core, half, x ^ (odd if core else even)))
        return lax.ppermute(array, PLANE, pairs)
    pairs = [(d * 8 + t, (d ^ (odd if t % 2 else even)) * 8 + t) for d in range(4) for t in range(8)]
    return lax.ppermute(array, ("dp", "tm"), pairs)


def to_core(array):
    return lax.ppermute(array, "tm", [(i, i ^ 1) for i in range(8)])


def to_z(array, step):
    return lax.ppermute(array, "tm", [(i, i ^ (2 * step)) for i in range(8)])


def to_dp(array, step):
    return lax.ppermute(array, "dp", [(i, i ^ step) for i in range(4)])


def to_half(array):
    return lax.ppermute(array, "patch", [(i, i ^ 4) for i in range(8)])


def after(values, done):
    return lax.optimization_barrier((values, done))[0]


def pick(array, index):
    return lax.dynamic_index_in_dim(array, index, 0, keepdims=False)


def dot(left, right, left_dim, right_dim):
    dims = (((left_dim,), (right_dim,)), ((), ()))
    return lax.dot_general(left, right, dims, preferred_element_type=f32)


def array(shape, kind):
    return jax.ShapeDtypeStruct(shape, kind)


def call(kernel, out, inputs, place, grid, in_specs, out_specs, scratch=(), mib=16):
    return pl.pallas_call(
        kernel,
        grid_spec=pltpu.PrefetchScalarGridSpec(
            num_scalar_prefetch=1,
            grid=grid,
            in_specs=in_specs,
            out_specs=out_specs,
            scratch_shapes=scratch,
        ),
        out_shape=out,
        compiler_params=pltpu.CompilerParams(vmem_limit_bytes=mib * 2**20),
        cost_estimate=pl.CostEstimate(flops=1, bytes_accessed=1, transcendentals=0),
    )(place, *inputs)


def whole(shape):
    return pl.BlockSpec(shape, lambda i, p: (0,) * len(shape))


def attention_kernel(place, *refs):
    scale = 1.0 / math.sqrt(HS)
    z, core = place[0], place[1]
    in_refs, out_refs = refs[:4], refs[4:]
    frames, columns = 16, in_refs[0].shape[1]
    rows = frames * columns

    def frame_of(index):
        slot = index // columns
        return ((slot // 4) ^ z) * 4 + (((slot % 4) // 2) ^ core) * 2 + slot % 2

    row = lax.broadcasted_iota(jnp.int32, (rows, 1), 0)
    col = lax.broadcasted_iota(jnp.int32, (1, rows), 1)
    allowed = (row % columns == col % columns) & (frame_of(row) >= frame_of(col))
    packed = jnp.concatenate([r[...] for r in in_refs], axis=0).reshape(rows, 8 * HS)
    for head in range(2):
        qkv = packed[:, 3 * head * HS : 3 * (head + 1) * HS]
        queries, keys, values = qkv[:, :HS], qkv[:, HS : 2 * HS], qkv[:, 2 * HS :]
        cot = packed[:, (6 + head) * HS : (7 + head) * HS]
        scores = dot(queries, keys, 1, 1) * scale
        exped = jnp.where(allowed, jnp.exp(scores), 0.0)
        probs = exped / jnp.sum(exped, axis=-1, keepdims=True)
        prob_grads = dot(cot, values, 1, 1)
        delta = jnp.sum(probs * prob_grads, axis=-1, keepdims=True)
        score_grads = (probs * (prob_grads - delta) * scale).astype(bf16)
        probs_low = probs.astype(bf16)
        grads = (
            dot(score_grads, keys, 1, 0),
            dot(score_grads, queries, 0, 0),
            dot(probs_low, cot, 0, 0),
            dot(probs_low, values, 1, 0),
        )
        out = jnp.concatenate([g.astype(bf16) for g in grads], axis=-1)
        out = out.reshape(4, 4, columns, 4 * HS)
        for i in range(4):
            out_refs[i][:, :, 4 * head * HS : 4 * (head + 1) * HS] = out[i]


def attention(place, packed):
    frames, patches, _ = packed[0].shape
    block = 16
    spec = lambda width: pl.BlockSpec((frames, block, width), lambda i, p: (0, i, 0))
    return call(
        attention_kernel,
        [array((frames, patches, 8 * HS), bf16)] * 4,
        packed,
        place,
        (patches // block,),
        [spec(8 * HS)] * 4,
        [spec(8 * HS)] * 4,
    )


def flip_tokens_kernel(place, *refs):
    refs[-1][...] = jnp.concatenate([r[...] for r in refs[:-1]], axis=0).T


def flip_tokens(place, pieces):
    tokens, width = pieces[0].shape
    quarter = width // 4
    return call(
        flip_tokens_kernel,
        [array((width, 4 * tokens), bf16)],
        pieces,
        place,
        (4,),
        [pl.BlockSpec((tokens, quarter), lambda i, p: (0, i))] * 4,
        [pl.BlockSpec((quarter, 4 * tokens), lambda i, p: (i, 0))],
    )[0]


def rows_of(i, place):
    return (place[1] ^ (i // 2)) * 2 + ((place[2] // 2) ^ (i % 2))


def far_specs(quarter):
    return [
        pl.BlockSpec((quarter, 4 * HS), lambda i, p: (jnp.minimum(i, 1), 0)),
        pl.BlockSpec((quarter, 4 * HS), lambda i, p: (jnp.maximum(i - 2, 0), 0)),
    ]


def far_rows(place, refs):
    run = refs[0].shape[0] // 2
    odd = place[2] % 2
    parts = []
    for start in (odd, 1 - odd):
        rows = pl.ds(pl.multiple_of(start * run, run), run)
        parts.append(jnp.where(pl.program_id(0) < 2, refs[0][rows, :], refs[1][rows, :]))
    return jnp.concatenate(parts, axis=0)


def project_kernel(place, *refs):
    tokens, weights, (mine_ref, theirs_ref, total) = refs[:8], refs[8:14], refs[14:]
    i = pl.program_id(0)
    normed = jnp.concatenate([r[...] for r in tokens[:4]], axis=0)
    cot = jnp.concatenate([r[...] for r in tokens[4:]], axis=0)
    far = far_rows(place, weights[4:])
    wide = jnp.concatenate([r[...] for r in weights[:3]] + [far[:, : 3 * HS]], axis=1)
    narrow = jnp.concatenate((weights[3][...].T, far[:, 3 * HS :]), axis=1)
    part = jnp.concatenate((dot(normed, wide, 1, 0), dot(cot, narrow, 1, 0)), axis=1)

    @pl.when(i == 0)
    def _():
        total[...] = part

    @pl.when(i > 0)
    def _():
        total[...] += part

    @pl.when(i == 3)
    def _():
        steps, frames, half, columns = mine_ref.shape
        out = total[...].astype(bf16).reshape(steps, frames, 2, half, columns)
        core = place[1]
        mine_ref[...] = jnp.where(core == 0, out[:, :, 0], out[:, :, 1])
        theirs_ref[...] = jnp.where(core == 0, out[:, :, 1], out[:, :, 0])


def project(place, frames, normed, cot, weights):
    rows, width = normed[0].shape
    quarter = width // 4
    specs = [pl.BlockSpec((quarter, HS), lambda i, p: (rows_of(i, p), 0))] * 3
    specs = specs + [pl.BlockSpec((HS, quarter), lambda i, p: (0, rows_of(i, p)))]
    out = (4, frames, rows // frames // 2, 8 * HS)
    return call(
        project_kernel,
        [array(out, bf16)] * 2,
        (*normed, *cot, *weights),
        place,
        (4,),
        [pl.BlockSpec((rows, quarter), lambda i, p: (0, rows_of(i, p)))] * 8
        + specs
        + far_specs(quarter),
        [whole(out)] * 2,
        [pltpu.VMEM((4 * rows, 8 * HS), f32)],
        56,
    )


def order(core):
    return 2, 1 + 2 * core, 3 - 2 * core, 0


def in_order(i, core):
    first = jnp.where(i == 0, 2, 0)
    return jnp.where(i == 1, 1 + 2 * core, jnp.where(i == 2, 3 - 2 * core, first))


def join_patches(core, mine_ref, other_ref, out_ref):
    half = mine_ref.shape[2]
    out_ref[:, :, pl.ds(pl.multiple_of(core * half, half), half), :] = mine_ref[...]
    out_ref[:, :, pl.ds(pl.multiple_of((1 - core) * half, half), half), :] = other_ref[...]


def weight_kernel(place, normed, cot, mine_ref, other_ref, out_ref, grads_ref, *, keep):
    side = place[1] if keep else 1 - place[1]

    @pl.when(pl.program_id(0) == 0)
    def _():
        join_patches(place[1], mine_ref, other_ref, grads_ref)

    grads = grads_ref[...].reshape(-1, 8 * HS)
    wide = 3 * HS

    def rows(ref):
        both = ref[...].reshape(4, 2, -1, ref.shape[-1])
        return jnp.where(side == 0, both[:, 0], both[:, 1]).reshape(-1, ref.shape[-1])

    by_normed = jnp.concatenate((grads[:, :wide], grads[:, 4 * HS : 7 * HS]), axis=1)
    by_cot = jnp.concatenate((grads[:, wide : 4 * HS], grads[:, 7 * HS :]), axis=1)
    by_normed = dot(rows(normed), by_normed, 1, 0).astype(out_ref.dtype)
    by_cot = dot(rows(cot), by_cot, 1, 0).astype(out_ref.dtype)
    for head in range(2):
        start = 4 * head * HS
        out_ref[0, :, start : start + wide] = by_normed[:, head * wide : (head + 1) * wide]
        out_ref[0, :, start + wide : start + 4 * HS] = by_cot[:, head * HS : (head + 1) * HS]


def weight_grads(place, normed, cot, mine, other, keep):
    width, tokens = normed.shape
    quarter = width // 4
    tokens_spec = pl.BlockSpec(
        (quarter, tokens), lambda i, p: (p[2] ^ in_order(i, p[1] if keep else 1 - p[1]), 0)
    )
    shape = (4, quarter // 2, 8 * HS)
    return call(
        functools.partial(weight_kernel, keep=keep),
        [array(shape, f32 if keep else bf16)],
        (normed, cot, mine, other),
        place,
        (4,),
        [tokens_spec] * 2 + [whole(mine.shape)] * 2,
        [pl.BlockSpec((1, *shape[1:]), lambda i, p: (i, 0, 0))],
        [pltpu.VMEM(mine.shape[:2] + (2 * mine.shape[2], 8 * HS), bf16)],
    )[0]


def token_kernel(place, *refs):
    mine_ref, other_ref, weights, outs, (grads_ref, left_ref) = refs[0], refs[1], refs[2:7], refs[7:11], refs[11:]
    core = place[1]
    rows = outs[0].shape[0]

    @pl.when(pl.program_id(0) == 0)
    def _():
        join_patches(core, mine_ref, other_ref, grads_ref)
        for i, step in enumerate(order(core)):
            piece = grads_ref[step].reshape(rows, 8 * HS)
            piece = jnp.concatenate((piece[:, : 3 * HS], piece[:, 4 * HS : 7 * HS]), axis=1)
            left_ref[i * rows : (i + 1) * rows, :] = piece

    near = [r[...] for r in weights[:3]]
    right = jnp.concatenate(near + [far_rows(place, weights[3:])[:, : 3 * HS]], axis=1)
    out = dot(left_ref[...], right.T, 1, 0)
    for i, ref in enumerate(outs):
        ref[...] = out[i * rows : (i + 1) * rows].astype(ref.dtype)


def token_grads(place, grads, near, far):
    _, frames, half, _ = grads[0].shape
    rows, width = 2 * frames * half, near[0].shape[0]
    quarter = width // 4
    return call(
        token_kernel,
        [array((rows, width), kind) for kind in (bf16, bf16, f32, f32)],
        (*grads, *near, *far),
        place,
        (4,),
        [whole(grads[0].shape)] * 2
        + [pl.BlockSpec((quarter, HS), lambda i, p: (rows_of(i, p), 0))] * 3
        + far_specs(quarter),
        [pl.BlockSpec((rows, quarter), lambda i, p: (0, rows_of(i, p)))] * 4,
        [
            pltpu.VMEM((4, frames, 2 * half, 8 * HS), bf16),
            pltpu.VMEM((4 * rows, 6 * HS), bf16),
        ],
    )


def shards(inputs, w_query, w_key, w_value, w_out, grad_out):
    _, frames, patches, width = inputs.shape
    tokens = frames * patches
    tm, patch, dp = lax.axis_index("tm"), lax.axis_index("patch"), lax.axis_index("dp")
    z, core, half, x = tm // 2, tm % 2, patch // 4, patch % 4
    place = jnp.stack((z, core, dp)).astype(jnp.int32)
    even = core == 0
    eighth = width // 8

    def choose(first, second):
        return jnp.where(even, first, second)

    def ring_start(opposite, direct, axis):
        return hop(opposite.astype(bf16), axis, 1, 3), hop(direct.astype(bf16), axis, 1, 3)

    def ring_end(relayed, direct, late, own, axis):
        late = hop((late + relayed.astype(f32)).astype(bf16), axis, 3, 1)
        return own + direct.astype(f32) + late.astype(f32)

    cot = grad_out.reshape(tokens, width)
    cot_1, cot_3 = hop(cot, "patch", 1, 1), hop(cot, "patch", 3, 3)

    start = core * 4 * eighth + dp * eighth
    part = [lax.dynamic_slice_in_dim(w, start, eighth, 0) for w in (w_query, w_key, w_value)]
    part = part + [lax.dynamic_slice_in_dim(w_out, start, eighth, 1).T]
    part = jnp.concatenate(part, axis=1)
    inputs = after(inputs, (part, place))
    part = to_half(part)

    wide_x = inputs.astype(f32)
    inverse = lax.rsqrt(jnp.mean(wide_x * wide_x, axis=-1, keepdims=True) + epsilon)
    normed_wide = wide_x * inverse
    normed = normed_wide.astype(bf16).reshape(tokens, width)

    normed_1, normed_3 = hop(normed, "patch", 1, 1), hop(normed, "patch", 3, 3)
    pieces = [part] + [to_dp(part, step) for step in (1, 2, 3)]
    cot_2 = after(choose(cot_3, cot_1), (pieces[1], pieces[3]))
    normed_2 = after(choose(normed_3, normed_1), cot_2)
    cot_2, normed_2 = hop(cot_2, "patch", 1, 3), hop(normed_2, "patch", 1, 3)
    got = jnp.concatenate(after(pieces, (cot_2, normed_2)), axis=0)
    far = (got, to_core(got))
    normed_pieces = (normed, normed_1, normed_2, normed_3)
    turn = z ^ x

    def scatter(mine, theirs):
        both = jnp.stack((mine, to_core(theirs)), axis=1)
        shape = (2 * frames, patches // 2, mine.shape[-1])
        pieces = [pick(both, turn ^ step).reshape(shape) for step in range(4)]
        return [pieces[0]] + [to_z(pieces[step], step) for step in (1, 2, 3)]

    near = (w_query, w_key, w_value)
    cot_pieces = (cot, cot_1, cot_2, cot_3)
    weights = (*near, w_out, *far)
    packed = scatter(*project(place, frames, normed_pieces, cot_pieces, weights))
    normed_flat = flip_tokens(after(place, packed[1]), normed_pieces)
    cot_flat = flip_tokens(after(place, normed_flat), cot_pieces)
    grads = attention(after(place, cot_flat), packed)

    back = jnp.stack([grads[0]] + [to_z(grads[step], step) for step in (1, 2, 3)])
    back = jnp.stack([pick(back, turn ^ step) for step in range(4)])
    back = back.reshape(4, 2, frames, patches // 2, 8 * HS)
    back = (back[:, 0], to_core(back[:, 1]))

    given = weight_grads(place, normed_flat, cot_flat, *back, False)
    kept = weight_grads(after(place, given), normed_flat, cot_flat, *back, True)
    given = after(to_core(given), kept)
    pieces = [kept[i] + given[i].astype(f32) for i in range(4)]
    pieces = [piece.astype(bf16) for piece in pieces[:2]] + pieces[2:]
    weights_way = ring_start(*pieces[:2], "dp")
    terms = token_grads(after(place, pieces), back, near, far)
    tokens_way = ring_start(*terms[:2], "patch")
    relayed = after(weights_way[0], terms)
    partial = ring_end(relayed, weights_way[1], *pieces[2:], "dp").astype(bf16)
    tokens_way = (after(tokens_way[0], relayed), tokens_way[1])
    grad_normed = ring_end(*tokens_way, *terms[2:], "patch").reshape(inputs.shape)

    def over_z(pieces):
        return [to_z(pick(pieces, z ^ step), step) for step in (1, 2, 3)]

    def sum_z(pieces, came):
        return sum((piece.astype(f32) for piece in came), pick(pieces, z).astype(f32))

    near_sums, far_sums = [
        partial[:, columns].reshape(4, eighth // 4, 4 * HS)
        for columns in (slice(0, 4 * HS), slice(4 * HS, 8 * HS))
    ]
    far_came = over_z(far_sums)
    near_sums = after(near_sums, far_came[0])
    near_came = over_z(near_sums)
    far_total = to_half(sum_z(far_sums, far_came).astype(bf16))
    reduced = sum_z(near_sums, near_came) + far_total.astype(f32)

    mean_term = jnp.mean(grad_normed * normed_wide, axis=-1, keepdims=True)
    grad_inputs = grad_out.astype(f32) + inverse * (grad_normed - normed_wide * mean_term)
    return (
        grad_inputs.astype(bf16),
        reduced[:, :HS],
        reduced[:, HS : 2 * HS],
        reduced[:, 2 * HS : 3 * HS],
        reduced[:, 3 * HS :].T,
    )


def solution(mesh):
    placed = (
        P("dp", "tm", "patch", None),
        P(None, "patch"),
        P(None, "patch"),
        P(None, "patch"),
        P("patch", None),
        P("dp", "tm", "patch", None),
    )
    return jax.shard_map(
        shards,
        mesh=mesh,
        in_specs=placed,
        out_specs=(
            P("dp", "tm", "patch", None),
            P(("dp", "tm"), "patch"),
            P(("dp", "tm"), "patch"),
            P(("dp", "tm"), "patch"),
            P("patch", ("dp", "tm")),
        ),
        check_vma=False,
    )
```

```python
import functools
import math

import jax
import jax.numpy as jnp
from jax import lax
from jax.experimental import pallas as pl
from jax.experimental.pallas import tpu as pltpu
from jax.sharding import PartitionSpec as P

HS = 128
epsilon = 1e-06
f32 = jnp.float32
bf16 = jnp.bfloat16
PLANE = ("tm", "patch")


def plane_pairs(target):
    pairs = []
    for z in range(4):
        for core in range(2):
            for half in range(2):
                for x in range(4):
                    goal = target(z, core, half, x)
                    if goal is not None:
                        tz, tcore, thalf, tx = goal
                        pairs.append(
                            ((z * 2 + core) * 8 + half * 4 + x, (tz * 2 + tcore) * 8 + thalf * 4 + tx)
                        )
    return pairs


def hop(array, axis, even, odd):
    if axis == "patch":
        pairs = plane_pairs(lambda z, core, half, x: (z, core, half, x ^ (odd if core else even)))
        return lax.ppermute(array, PLANE, pairs)
    pairs = [(d * 8 + t, (d ^ (odd if t % 2 else even)) * 8 + t) for d in range(4) for t in range(8)]
    return lax.ppermute(array, ("dp", "tm"), pairs)


def to_core(array):
    return lax.ppermute(array, "tm", [(i, i ^ 1) for i in range(8)])


def to_z(array, step):
    return lax.ppermute(array, "tm", [(i, i ^ (2 * step)) for i in range(8)])


def to_dp(array, step):
    return lax.ppermute(array, "dp", [(i, i ^ step) for i in range(4)])


def to_half(array):
    return lax.ppermute(array, "patch", [(i, i ^ 4) for i in range(8)])


def after(values, done):
    return lax.optimization_barrier((values, done))[0]


def pick(array, index):
    return lax.dynamic_index_in_dim(array, index, 0, keepdims=False)


def dot(left, right, left_dim, right_dim):
    dims = (((left_dim,), (right_dim,)), ((), ()))
    return lax.dot_general(left, right, dims, preferred_element_type=f32)


def array(shape, kind):
    return jax.ShapeDtypeStruct(shape, kind)


def call(kernel, out, inputs, place, grid, in_specs, out_specs, scratch=(), mib=16):
    return pl.pallas_call(
        kernel,
        grid_spec=pltpu.PrefetchScalarGridSpec(
            num_scalar_prefetch=1,
            grid=grid,
            in_specs=in_specs,
            out_specs=out_specs,
            scratch_shapes=scratch,
        ),
        out_shape=out,
        compiler_params=pltpu.CompilerParams(vmem_limit_bytes=mib * 2**20),
        cost_estimate=pl.CostEstimate(flops=1, bytes_accessed=1, transcendentals=0),
    )(place, *inputs)


def whole(shape):
    return pl.BlockSpec(shape, lambda i, p: (0,) * len(shape))


def attention_kernel(place, *refs):
    scale = 1.0 / math.sqrt(HS)
    z, core = place[0], place[1]
    in_refs, out_refs = refs[:4], refs[4:]
    frames, columns = 16, in_refs[0].shape[1]
    rows = frames * columns

    def frame_of(index):
        slot = index // columns
        return ((slot // 4) ^ z) * 4 + (((slot % 4) // 2) ^ core) * 2 + slot % 2

    row = lax.broadcasted_iota(jnp.int32, (rows, 1), 0)
    col = lax.broadcasted_iota(jnp.int32, (1, rows), 1)
    allowed = (row % columns == col % columns) & (frame_of(row) >= frame_of(col))
    packed = jnp.concatenate([r[...] for r in in_refs], axis=0).reshape(rows, 8 * HS)
    for head in range(2):
        qkv = packed[:, 3 * head * HS : 3 * (head + 1) * HS]
        queries, keys, values = qkv[:, :HS], qkv[:, HS : 2 * HS], qkv[:, 2 * HS :]
        cot = packed[:, (6 + head) * HS : (7 + head) * HS]
        scores = dot(queries, keys, 1, 1) * scale
        exped = jnp.where(allowed, jnp.exp(scores), 0.0)
        probs = exped / jnp.sum(exped, axis=-1, keepdims=True)
        prob_grads = dot(cot, values, 1, 1)
        delta = jnp.sum(probs * prob_grads, axis=-1, keepdims=True)
        score_grads = (probs * (prob_grads - delta) * scale).astype(bf16)
        probs_low = probs.astype(bf16)
        grads = (
            dot(score_grads, keys, 1, 0),
            dot(score_grads, queries, 0, 0),
            dot(probs_low, cot, 0, 0),
            dot(probs_low, values, 1, 0),
        )
        out = jnp.concatenate([g.astype(bf16) for g in grads], axis=-1)
        out = out.reshape(4, 4, columns, 4 * HS)
        for i in range(4):
            out_refs[i][:, :, 4 * head * HS : 4 * (head + 1) * HS] = out[i]


def attention(place, packed):
    frames, patches, _ = packed[0].shape
    block = 16
    spec = lambda width: pl.BlockSpec((frames, block, width), lambda i, p: (0, i, 0))
    return call(
        attention_kernel,
        [array((frames, patches, 8 * HS), bf16)] * 4,
        packed,
        place,
        (patches // block,),
        [spec(8 * HS)] * 4,
        [spec(8 * HS)] * 4,
    )


def flip_tokens_kernel(place, *refs):
    refs[-1][...] = jnp.concatenate([r[...] for r in refs[:-1]], axis=0).T


def flip_tokens(place, pieces):
    tokens, width = pieces[0].shape
    quarter = width // 4
    return call(
        flip_tokens_kernel,
        [array((width, 4 * tokens), bf16)],
        pieces,
        place,
        (4,),
        [pl.BlockSpec((tokens, quarter), lambda i, p: (0, i))] * 4,
        [pl.BlockSpec((quarter, 4 * tokens), lambda i, p: (i, 0))],
    )[0]


def rows_of(i, place):
    return (place[1] ^ (i // 2)) * 2 + ((place[2] // 2) ^ (i % 2))


def far_specs(quarter):
    return [
        pl.BlockSpec((quarter, 4 * HS), lambda i, p: (jnp.minimum(i, 1), 0)),
        pl.BlockSpec((quarter, 4 * HS), lambda i, p: (0, 0)),
        pl.BlockSpec((quarter, 4 * HS), lambda i, p: (0, 0)),
    ]


def far_rows(place, refs):
    run = refs[0].shape[0] // 2
    odd = place[2] % 2
    parts = []
    for start in (odd, 1 - odd):
        rows = pl.ds(pl.multiple_of(start * run, run), run)
        other = jnp.where(pl.program_id(0) == 2, refs[1][rows, :], refs[2][rows, :])
        parts.append(jnp.where(pl.program_id(0) < 2, refs[0][rows, :], other))
    return jnp.concatenate(parts, axis=0)


def project_kernel(place, *refs):
    tokens, weights, (mine_ref, theirs_ref, total) = refs[:8], refs[8:15], refs[15:]
    i = pl.program_id(0)
    normed = jnp.concatenate([r[...] for r in tokens[:4]], axis=0)
    cot = jnp.concatenate([r[...] for r in tokens[4:]], axis=0)
    far = far_rows(place, weights[4:])
    wide = jnp.concatenate([r[...] for r in weights[:3]] + [far[:, : 3 * HS]], axis=1)
    narrow = jnp.concatenate((weights[3][...].T, far[:, 3 * HS :]), axis=1)
    part = jnp.concatenate((dot(normed, wide, 1, 0), dot(cot, narrow, 1, 0)), axis=1)

    @pl.when(i == 0)
    def _():
        total[...] = part

    @pl.when(i > 0)
    def _():
        total[...] += part

    @pl.when(i == 3)
    def _():
        steps, frames, half, columns = mine_ref.shape
        out = total[...].astype(bf16).reshape(steps, frames, 2, half, columns)
        core = place[1]
        mine_ref[...] = jnp.where(core == 0, out[:, :, 0], out[:, :, 1])
        theirs_ref[...] = jnp.where(core == 0, out[:, :, 1], out[:, :, 0])


def project(place, frames, normed, cot, weights):
    rows, width = normed[0].shape
    quarter = width // 4
    specs = [pl.BlockSpec((quarter, HS), lambda i, p: (rows_of(i, p), 0))] * 3
    specs = specs + [pl.BlockSpec((HS, quarter), lambda i, p: (0, rows_of(i, p)))]
    out = (4, frames, rows // frames // 2, 8 * HS)
    return call(
        project_kernel,
        [array(out, bf16)] * 2,
        (*normed, *cot, *weights),
        place,
        (4,),
        [pl.BlockSpec((rows, quarter), lambda i, p: (0, rows_of(i, p)))] * 8
        + specs
        + far_specs(quarter),
        [whole(out)] * 2,
        [pltpu.VMEM((4 * rows, 8 * HS), f32)],
        56,
    )


def order(core):
    return 2, 1 + 2 * core, 3 - 2 * core, 0


def in_order(i, core):
    first = jnp.where(i == 0, 2, 0)
    return jnp.where(i == 1, 1 + 2 * core, jnp.where(i == 2, 3 - 2 * core, first))


def join_patches(core, mine_ref, other_ref, out_ref):
    half = mine_ref.shape[2]
    out_ref[:, :, pl.ds(pl.multiple_of(core * half, half), half), :] = mine_ref[...]
    out_ref[:, :, pl.ds(pl.multiple_of((1 - core) * half, half), half), :] = other_ref[...]


def weight_kernel(place, normed, cot, mine_ref, other_ref, out_ref, grads_ref, *, keep):
    side = place[1] if keep else 1 - place[1]

    @pl.when(pl.program_id(0) == 0)
    def _():
        join_patches(place[1], mine_ref, other_ref, grads_ref)

    grads = grads_ref[...].reshape(-1, 8 * HS)
    wide = 3 * HS

    def rows(ref):
        both = ref[...].reshape(4, 2, -1, ref.shape[-1])
        return jnp.where(side == 0, both[:, 0], both[:, 1]).reshape(-1, ref.shape[-1])

    by_normed = jnp.concatenate((grads[:, :wide], grads[:, 4 * HS : 7 * HS]), axis=1)
    by_cot = jnp.concatenate((grads[:, wide : 4 * HS], grads[:, 7 * HS :]), axis=1)
    by_normed = dot(rows(normed), by_normed, 1, 0).astype(out_ref.dtype)
    by_cot = dot(rows(cot), by_cot, 1, 0).astype(out_ref.dtype)
    for head in range(2):
        start = 4 * head * HS
        out_ref[0, :, start : start + wide] = by_normed[:, head * wide : (head + 1) * wide]
        out_ref[0, :, start + wide : start + 4 * HS] = by_cot[:, head * HS : (head + 1) * HS]


def weight_grads(place, normed, cot, mine, other, keep):
    width, tokens = normed.shape
    quarter = width // 4
    tokens_spec = pl.BlockSpec(
        (quarter, tokens), lambda i, p: (p[2] ^ in_order(i, p[1] if keep else 1 - p[1]), 0)
    )
    shape = (4, quarter // 2, 8 * HS)
    return call(
        functools.partial(weight_kernel, keep=keep),
        [array(shape, f32 if keep else bf16)],
        (normed, cot, mine, other),
        place,
        (4,),
        [tokens_spec] * 2 + [whole(mine.shape)] * 2,
        [pl.BlockSpec((1, *shape[1:]), lambda i, p: (i, 0, 0))],
        [pltpu.VMEM(mine.shape[:2] + (2 * mine.shape[2], 8 * HS), bf16)],
    )[0]


def token_kernel(place, *refs):
    mine_ref, other_ref, weights, outs, (grads_ref, left_ref) = refs[0], refs[1], refs[2:8], refs[8:12], refs[12:]
    core = place[1]
    rows = outs[0].shape[0]

    @pl.when(pl.program_id(0) == 0)
    def _():
        join_patches(core, mine_ref, other_ref, grads_ref)
        for i, step in enumerate(order(core)):
            piece = grads_ref[step].reshape(rows, 8 * HS)
            piece = jnp.concatenate((piece[:, : 3 * HS], piece[:, 4 * HS : 7 * HS]), axis=1)
            left_ref[i * rows : (i + 1) * rows, :] = piece

    near = [r[...] for r in weights[:3]]
    right = jnp.concatenate(near + [far_rows(place, weights[3:])[:, : 3 * HS]], axis=1)
    out = dot(left_ref[...], right.T, 1, 0)
    for i, ref in enumerate(outs):
        ref[...] = out[i * rows : (i + 1) * rows].astype(ref.dtype)


def token_grads(place, grads, near, far):
    _, frames, half, _ = grads[0].shape
    rows, width = 2 * frames * half, near[0].shape[0]
    quarter = width // 4
    return call(
        token_kernel,
        [array((rows, width), kind) for kind in (bf16, bf16, f32, f32)],
        (*grads, *near, *far),
        place,
        (4,),
        [whole(grads[0].shape)] * 2
        + [pl.BlockSpec((quarter, HS), lambda i, p: (rows_of(i, p), 0))] * 3
        + far_specs(quarter),
        [pl.BlockSpec((rows, quarter), lambda i, p: (0, rows_of(i, p)))] * 4,
        [
            pltpu.VMEM((4, frames, 2 * half, 8 * HS), bf16),
            pltpu.VMEM((4 * rows, 6 * HS), bf16),
        ],
    )


def shards(inputs, w_query, w_key, w_value, w_out, grad_out):
    _, frames, patches, width = inputs.shape
    tokens = frames * patches
    tm, patch, dp = lax.axis_index("tm"), lax.axis_index("patch"), lax.axis_index("dp")
    z, core, half, x = tm // 2, tm % 2, patch // 4, patch % 4
    place = jnp.stack((z, core, dp)).astype(jnp.int32)
    even = core == 0
    eighth = width // 8

    def choose(first, second):
        return jnp.where(even, first, second)

    def ring_start(opposite, direct, axis):
        return hop(opposite.astype(bf16), axis, 1, 3), hop(direct.astype(bf16), axis, 1, 3)

    def ring_end(relayed, direct, late, own, axis):
        late = hop((late + relayed.astype(f32)).astype(bf16), axis, 3, 1)
        return own + direct.astype(f32) + late.astype(f32)

    cot = grad_out.reshape(tokens, width)
    cot_1, cot_3 = hop(cot, "patch", 1, 1), hop(cot, "patch", 3, 3)

    start = core * 4 * eighth + dp * eighth
    part = [lax.dynamic_slice_in_dim(w, start, eighth, 0) for w in (w_query, w_key, w_value)]
    part = part + [lax.dynamic_slice_in_dim(w_out, start, eighth, 1).T]
    part = jnp.concatenate(part, axis=1)
    inputs = after(inputs, (part, place))
    part = to_half(part)

    wide_x = inputs.astype(f32)
    inverse = lax.rsqrt(jnp.mean(wide_x * wide_x, axis=-1, keepdims=True) + epsilon)
    normed_wide = wide_x * inverse
    normed = normed_wide.astype(bf16).reshape(tokens, width)

    normed_1, normed_3 = hop(normed, "patch", 1, 1), hop(normed, "patch", 3, 3)
    pieces = [part] + [to_dp(part, step) for step in (1, 2, 3)]
    relayed = jnp.concatenate((choose(cot_3, cot_1), choose(normed_3, normed_1)), axis=0)
    relayed = after(relayed, (pieces[1], pieces[3]))
    got = jnp.concatenate(after(pieces, relayed), axis=0)
    relayed = hop(relayed, "patch", 1, 3)
    cot_2, normed_2 = relayed[:tokens], relayed[tokens:]
    far = (got, to_core(got[: 2 * eighth]), to_core(got[2 * eighth :]))
    normed_pieces = (normed, normed_1, normed_2, normed_3)
    turn = z ^ x

    def scatter(mine, theirs):
        both = jnp.stack((mine, to_core(theirs)), axis=1)
        shape = (2 * frames, patches // 2, mine.shape[-1])
        pieces = [pick(both, turn ^ step).reshape(shape) for step in range(4)]
        return [pieces[0]] + [to_z(pieces[step], step) for step in (1, 2, 3)]

    near = (w_query, w_key, w_value)
    cot_pieces = (cot, cot_1, cot_2, cot_3)
    weights = (*near, w_out, *far)
    packed = scatter(*project(place, frames, normed_pieces, cot_pieces, weights))
    normed_flat = flip_tokens(after(place, packed[1]), normed_pieces)
    cot_flat = flip_tokens(after(place, normed_flat), cot_pieces)
    grads = attention(after(place, cot_flat), packed)

    back = jnp.stack([grads[0]] + [to_z(grads[step], step) for step in (1, 2, 3)])
    back = jnp.stack([pick(back, turn ^ step) for step in range(4)])
    back = back.reshape(4, 2, frames, patches // 2, 8 * HS)
    back = (back[:, 0], to_core(back[:, 1]))

    given = weight_grads(place, normed_flat, cot_flat, *back, False)
    kept = weight_grads(after(place, given), normed_flat, cot_flat, *back, True)
    given = after(to_core(given), kept)
    pieces = [kept[i] + given[i].astype(f32) for i in range(4)]
    pieces = [piece.astype(bf16) for piece in pieces[:2]] + pieces[2:]
    weights_way = ring_start(*pieces[:2], "dp")
    terms = token_grads(after(place, pieces), back, near, far)
    tokens_way = ring_start(*terms[:2], "patch")
    relayed = after(weights_way[0], terms)
    partial = ring_end(relayed, weights_way[1], *pieces[2:], "dp").astype(bf16)
    tokens_way = (after(tokens_way[0], relayed), tokens_way[1])
    grad_normed = ring_end(*tokens_way, *terms[2:], "patch").reshape(inputs.shape)

    def over_z(pieces):
        return [to_z(pick(pieces, z ^ step), step) for step in (1, 2, 3)]

    def sum_z(pieces, came):
        return sum((piece.astype(f32) for piece in came), pick(pieces, z).astype(f32))

    near_sums, far_sums = [
        partial[:, columns].reshape(4, eighth // 4, 4 * HS)
        for columns in (slice(0, 4 * HS), slice(4 * HS, 8 * HS))
    ]
    far_came = over_z(far_sums)
    near_sums = after(near_sums, far_came[0])
    near_came = over_z(near_sums)
    far_total = to_half(sum_z(far_sums, far_came).astype(bf16))
    reduced = sum_z(near_sums, near_came) + far_total.astype(f32)

    mean_term = jnp.mean(grad_normed * normed_wide, axis=-1, keepdims=True)
    grad_inputs = grad_out.astype(f32) + inverse * (grad_normed - normed_wide * mean_term)
    return (
        grad_inputs.astype(bf16),
        reduced[:, :HS],
        reduced[:, HS : 2 * HS],
        reduced[:, 2 * HS : 3 * HS],
        reduced[:, 3 * HS :].T,
    )


def solution(mesh):
    placed = (
        P("dp", "tm", "patch", None),
        P(None, "patch"),
        P(None, "patch"),
        P(None, "patch"),
        P("patch", None),
        P("dp", "tm", "patch", None),
    )
    return jax.shard_map(
        shards,
        mesh=mesh,
        in_specs=placed,
        out_specs=(
            P("dp", "tm", "patch", None),
            P(("dp", "tm"), "patch"),
            P(("dp", "tm"), "patch"),
            P(("dp", "tm"), "patch"),
            P("patch", ("dp", "tm")),
        ),
        check_vma=False,
    )
```
